256 devices in a mesh: orb: 32 (over z, x), slab: 8 (over y, core).
Axes of the slice: x: 4, y: 4, z: 8, core: 2. Of those that a mesh axis runs over, the one named last changes fastest.
Arguments:
- orbitals: bfloat16 [32, 64, 64, 128], P('orb', 'slab'), may hold values from -6 to 6
- pair_table: int32 [1024, 3], P('orb'), may hold values from -1 to 31, as said below
Outputs:
- exchange_action: float32 [32, 64, 64, 128], P('orb', 'slab')
The draws below stay inside these ranges and needn't reach their ends.
Inputs may be any that keep to these rules, and one draw needn't show every extreme that they name: `pair_table`: A live slot holds (m, n, s) with m <= n and s in 0, 1; an empty slot holds -1 in all three columns. A block of 32 slots has its live slots first. No (m, n, s) appears twice in the table. Exactly 528 slots are live, and the 32 blocks hold, in some order, k * 1 live slots for k = 1 to 32.
All inputs are finite; a program needn't handle non-finite values.
Results may differ from the reference program's by a relative error of at most 0.0003.
Values may be sent and summed in bfloat16 or wider, within the bound.
No kernel may reach another device: no remote copies, remote signals or barrier semaphores. Data moves between devices by JAX's collectives and lax.ppermute only.
A program may use at most 64 MiB of HBM per device.

```python
import math
import jax
import jax.numpy as jnp
from jax import lax

G = 64
CP_DEV = 1
COUPLES = 32
N_ORB = 32


def draw_pair_table(key, part):
    couples = CP_DEV * N_ORB
    capacity = couples
    blocks = N_ORB
    upper_rows, upper_cols = jnp.triu_indices(couples)
    combos = upper_rows.shape[0] * 2
    shuffled = jax.random.permutation(jax.random.fold_in(key, 11), combos)
    ranking = jax.random.permutation(jax.random.fold_in(key, 12), blocks)
    counts = capacity * (ranking + 1) // blocks
    starts = jnp.cumsum(counts) - counts
    slot_index = jnp.arange(blocks * capacity, dtype=jnp.int32)
    block_of = slot_index // capacity
    column = slot_index % capacity
    is_live = column < counts[block_of]
    chosen = shuffled[jnp.where(is_live, starts[block_of] + column, 0)]
    pair_index = chosen // 2
    result_rows = jnp.stack([upper_rows[pair_index], upper_cols[pair_index], chosen % 2], axis=1).astype(jnp.int32)
    return jnp.where(is_live[:, None], result_rows, -1).astype(jnp.int32)


def steps_of(rng, extent, split, least, largest):
    level, own = 1.0, jax.random.fold_in(rng, 6)
    for dim, blocks in split:
        draws = jnp.exp(jax.random.uniform(jax.random.fold_in(own, dim), (blocks,), jnp.float32, least / len(split), largest / len(split)))
        level = level * jnp.repeat(draws, extent[dim] // blocks).reshape([-1 if axis == dim else 1 for axis in range(len(extent))])
    return level


def scatter_about(key, extent, deviation, bound, split=(), kind=jnp.bfloat16):
    gain = steps_of(key, extent, split, -0.22, 0.18) if split else 1.0
    array = jax.random.normal(key, extent, jnp.float32) * deviation * gain
    return jnp.minimum(jnp.maximum(array, -bound), bound).astype(kind)


def setup_inputs(seed: int = 0) -> dict:
    streams_of = jax.random.split(jax.random.key(seed), 3)
    orbitals = scatter_about(streams_of[0], (COUPLES, G, G, 2 * G), 1.0, 6.0, ((0, 32), (1, 8)))
    pair_table = draw_pair_table(jax.random.fold_in(streams_of[2], 71), 0)
    return dict(orbitals=orbitals, pair_table=pair_table)


exchange_fraction = 0.25
cell_ratio = 8.0


def folded(values, grid_len):
    return jnp.minimum(values, grid_len - values)


def kernel_half(grid_len):
    full_axis = folded(jnp.arange(grid_len, dtype=jnp.int32), grid_len).astype(jnp.float32)
    planes_x = cell_ratio * full_axis
    half_axis = jnp.arange(grid_len // 2 + 1, dtype=jnp.int32).astype(jnp.float32)
    scale_k = (2.0 * math.pi / grid_len) * (2.0 * math.pi / grid_len)
    squared = scale_k * (planes_x[:, None, None] * planes_x[:, None, None]
                         + full_axis[None, :, None] * full_axis[None, :, None]
                         + half_axis[None, None, :] * half_axis[None, None, :])
    safe_sq = jnp.where(squared > 0, squared, 1.0)
    return jnp.where(squared > 0, -exchange_fraction / safe_sq, 0.0)


def lane_swap(field_in, grid_len):
    return jnp.concatenate([field_in[..., grid_len:], field_in[..., :grid_len]], axis=-1)


def to_lanes(field_in, grid_len):
    return field_in.reshape(grid_len, grid_len, 2, grid_len).transpose(2, 0, 1, 3)


def from_lanes(field_in, grid_len):
    return field_in.transpose(1, 2, 0, 3).reshape(grid_len, grid_len, 2 * grid_len)


def reference(orbitals, pair_table):
    couples = orbitals.shape[0]
    grid_len = orbitals.shape[1]
    kernel = kernel_half(grid_len)

    def add_slot(totals, row_vals):
        first_id = row_vals[0]
        second_id = row_vals[1]
        left_rows = orbitals[first_id].astype(jnp.float32)
        right_rows = orbitals[second_id].astype(jnp.float32)
        partner = jnp.where(row_vals[2] == 1, lane_swap(right_rows, grid_len), right_rows)
        density = to_lanes(left_rows * partner, grid_len)
        spectrum = jnp.fft.rfftn(density, axes=(1, 2, 3))
        potential = jnp.fft.irfftn(spectrum * kernel[None], s=(grid_len, grid_len, grid_len), axes=(1, 2, 3))
        potential = from_lanes(potential.astype(left_rows.dtype), grid_len)
        first_term = potential * partner
        second_term = potential * left_rows
        second_term = jnp.where(row_vals[2] == 1, lane_swap(second_term, grid_len), second_term)
        totals = totals.at[first_id].add(first_term)
        return totals.at[second_id].add(jnp.where(first_id != second_id, second_term, 0.0))

    def visit(slot_index, totals):
        row_vals = pair_table[slot_index]
        return lax.cond(row_vals[0] >= 0, lambda acc_in: add_slot(acc_in, row_vals), lambda acc_in: acc_in, totals)

    totals = lax.fori_loop(0, pair_table.shape[0], visit, jnp.zeros(orbitals.shape, jnp.float32))
    orbital_count = 2 * couples
    cell_count = grid_len * grid_len * grid_len
    orbital_grid = orbitals.astype(jnp.float32).reshape(couples, grid_len, grid_len, 2, grid_len)
    orbital_grid = orbital_grid.transpose(0, 3, 1, 2, 4).reshape(orbital_count, cell_count)
    actions = totals.reshape(couples, grid_len, grid_len, 2, grid_len)
    actions = actions.transpose(0, 3, 1, 2, 4).reshape(orbital_count, cell_count)
    intersection = lax.dot_general(orbital_grid, actions, (((1,), (1,)), ((), ())), precision=lax.Precision.HIGHEST) / cell_count
    corrected = actions - lax.dot_general(intersection, orbital_grid, (((0,), (0,)), ((), ())), precision=lax.Precision.HIGHEST)
    corrected = corrected.reshape(couples, 2, grid_len, grid_len, grid_len).transpose(0, 2, 3, 1, 4)
    return corrected.reshape(orbitals.shape)
```

```python
import functools
import math

import jax
import jax.numpy as jnp
import ml_dtypes
import numpy as np
from jax import lax
from jax.experimental import pallas as pl
from jax.experimental.pallas import tpu as pltpu
from jax.sharding import Mesh
from jax.sharding import PartitionSpec as P

G = 64
ROWS = 2048
CHUNK = 256
KY_STEP = 4
NZ, NX, NY = 8, 4, 4
COUPLES = 32
CELLS = G * G * G
exchange_fraction = 0.25
cell_ratio = 8.0
f32, bf16 = jnp.float32, jnp.bfloat16


def split_np(mat):
    high = mat.astype(ml_dtypes.bfloat16)
    low = (mat - high.astype(np.float64)).astype(ml_dtypes.bfloat16)
    return high, low


def plane_order():
    r = np.arange(32)
    return [16 * (r // 8) + 8 * h + r % 8 for h in (0, 1)]


def weights():
    idx = np.arange(G)
    angles = 2.0 * np.pi / G * (idx[:, None] * idx[None, :] % G)
    hart = (np.cos(angles) + np.sin(angles)) / math.sqrt(G)
    high, low = split_np(np.kron(np.eye(2), hart))
    zero = np.zeros_like(high)
    w_depth = np.block([[high, low], [high, zero]])
    w_rows = np.block([[high, high], [low, zero]])
    s0, s1 = plane_order()
    mix = np.block(
        [
            [hart[np.ix_(s0, s0)], hart[np.ix_(s0, s1)]],
            [hart[np.ix_(s1, s1)], hart[np.ix_(s1, s0)]],
        ]
    )
    high, low = split_np(mix)
    w_planes = np.block([[high, high], [low, np.zeros_like(high)]])
    return w_depth, w_rows, w_planes


def coulomb():
    def folded(v):
        return jnp.minimum(v, G - v).astype(f32)

    lane = lax.broadcasted_iota(jnp.int32, (G, 32, 128), 2)
    row = lax.broadcasted_iota(jnp.int32, (G, 32, 128), 1)
    ky = folded(lax.broadcasted_iota(jnp.int32, (G, 32, 128), 0))
    kx = cell_ratio * folded(16 * (row // 8) + 8 * (lane // G) + row % 8)
    kz = folded(lane % G)
    scale = (2.0 * math.pi / G) * (2.0 * math.pi / G)
    squared = scale * (kx * kx + ky * ky + kz * kz)
    safe = jnp.where(squared > 0, squared, 1.0)
    return jnp.where(squared > 0, -exchange_fraction / safe, 0.0)


def assign_kernel(me_ref, code_ref, out_ref, load_ref):
    me = me_ref[0]

    def clear(i, carry):
        load_ref[i] = 0
        return carry

    lax.fori_loop(0, NZ * NX * NY, clear, 0)
    for i in range(17):
        out_ref[i] = 0

    def one_block(b, count):
        def live(state):
            s, _ = state
            return (s < 32) & (code_ref[b, jnp.minimum(s, 31)] >= 0)

        def step(state):
            s, cnt = state
            code = code_ref[b, s]
            m = code & 31
            n = (code >> 5) & 31
            flip = code >> 10
            mz, mx, nz, nx = m >> 2, m & 3, n >> 2, n & 3
            first = mz * 16 + nx * 4 + (nz >> 1)
            second = nz * 16 + mx * 4 + (mz >> 1)
            load_a = load_ref[first]
            load_b = load_ref[second]
            use_a = load_a <= load_b
            chip = jnp.where(use_a, first, second)
            load_ref[chip] = jnp.where(use_a, load_a, load_b) + 1
            task_a = mx + 4 * (nz & 1)
            task_b = nx + 4 * (mz & 1)
            task = jnp.where(use_a, task_a, task_b) + 8 * flip + 16 * (m == n).astype(jnp.int32)
            mine = chip == me

            @pl.when(mine)
            def _():
                out_ref[1 + cnt] = task

            return s + 1, cnt + mine.astype(jnp.int32)

        return lax.while_loop(live, step, (0, count))[1]

    out_ref[0] = lax.fori_loop(0, 32, one_block, 0)


def split(value):
    high = value.astype(bf16)
    return high, (value - high.astype(f32)).astype(bf16)


def depth_transform(value, w_depth):
    high, low = split(value)
    out = jnp.dot(jnp.concatenate([high, low], axis=1), w_depth, preferred_element_type=f32)
    return out[:, :128] + out[:, 128:]


def rows_transform(value, w_rows):
    high, low = split(value)
    half = CHUNK // 2
    top = jnp.concatenate([high[:half], high[half:]], axis=1)
    bottom = jnp.concatenate([low[:half], low[half:]], axis=1)
    out = jnp.dot(w_rows, jnp.concatenate([top, bottom], axis=0), preferred_element_type=f32)
    out = out[:half] + out[half:]
    return jnp.concatenate([out[:, :128], out[:, 128:]], axis=0)


def planes_transform(value, w_planes, low_lanes):
    turned = jnp.concatenate(
        [pltpu.roll(value[:, j * 128 : (j + 1) * 128], G, 1) for j in range(KY_STEP)], axis=1
    )
    vh, vl = split(value)
    th, tl = split(turned)
    out = jnp.dot(w_planes, jnp.concatenate([vh, th, vl, tl], axis=0), preferred_element_type=f32)
    out = out[:64] + out[64:]
    return jnp.where(low_lanes, out[:32], out[32:])


def pairs_kernel(lane_ref, tasks_ref, left_ref, right_ref, wz_ref, wy_ref, wx_ref, kern_ref, lacc_ref, racc_ref, t_ref):
    def clear(i, carry):
        rows = pl.ds(pl.multiple_of(i * CHUNK, CHUNK), CHUNK)
        for k in range(4):
            lacc_ref[k, rows] = jnp.zeros((CHUNK, 128), f32)
            racc_ref[k, rows] = jnp.zeros((CHUNK, 128), f32)
        return carry

    lax.fori_loop(0, ROWS // CHUNK, clear, 0)
    lane = lane_ref[0]
    low_lanes = lax.broadcasted_iota(jnp.int32, (32, KY_STEP * 128), 1) % 128 < G

    def one_task(t, carry):
        task = tasks_ref[1 + t]
        a = task & 3
        flip = (task >> 3) & 1
        b = (lane ^ flip) * 2 + ((task >> 2) & 1)
        second = 1.0 - (task >> 4).astype(f32)

        def forward(i, c):
            rows = pl.ds(pl.multiple_of(i * CHUNK, CHUNK), CHUNK)
            rho = left_ref[a, rows].astype(f32) * right_ref[b, rows].astype(f32)
            t_ref[rows] = rows_transform(depth_transform(rho, wz_ref[...]), wy_ref[...])
            return c

        lax.fori_loop(0, ROWS // CHUNK, forward, 0, unroll=2)

        def middle(i, c):
            first = i * KY_STEP
            value = jnp.concatenate(
                [t_ref[pl.ds(first + j, 32, stride=G)] for j in range(KY_STEP)], axis=1
            )
            kern = jnp.concatenate([kern_ref[first + j] for j in range(KY_STEP)], axis=1)
            value = planes_transform(value, wx_ref[...], low_lanes) * kern
            value = planes_transform(value, wx_ref[...], low_lanes)
            for j in range(KY_STEP):
                t_ref[pl.ds(first + j, 32, stride=G)] = value[:, j * 128 : (j + 1) * 128]
            return c

        lax.fori_loop(0, G // KY_STEP, middle, 0, unroll=2)

        def backward(i, c):
            rows = pl.ds(pl.multiple_of(i * CHUNK, CHUNK), CHUNK)
            v = depth_transform(rows_transform(t_ref[rows], wy_ref[...]), wz_ref[...])
            lacc_ref[a, rows] += v * right_ref[b, rows].astype(f32)
            racc_ref[b, rows] += (v * second) * left_ref[a, rows].astype(f32)
            return c

        lax.fori_loop(0, ROWS // CHUNK, backward, 0, unroll=2)
        return carry

    lax.fori_loop(0, tasks_ref[0], one_task, 0)


def overlap_kernel(x_ref, phi_ref, out_ref, turned_ref):
    for i in range(8):
        turned_ref[pl.ds(i * 64, 64)] = pltpu.roll(x_ref[pl.ds(i * 64, 64)], G, 1)

    def one(o, carry):
        same = jnp.zeros((64, 128), f32)
        cross = jnp.zeros((64, 128), f32)
        for i in range(8):
            rows = pl.ds(i * 64, 64)
            phi = phi_ref[o, rows].astype(f32)
            same = same + phi * x_ref[rows]
            cross = cross + phi * turned_ref[rows]
        out_ref[o, 0:1] = jnp.sum(same, axis=0, keepdims=True)
        out_ref[o, 1:2] = jnp.sum(cross, axis=0, keepdims=True)
        return carry

    lax.fori_loop(0, COUPLES, one, 0)


def project_kernel(x_ref, phi_ref, over_ref, out_ref, coef_ref):
    lane = lax.broadcasted_iota(jnp.int32, (COUPLES, 128), 1)
    for k in range(2):
        part = over_ref[:, k]
        low = jnp.sum(jnp.where(lane < G, part, 0.0), axis=1, keepdims=True)
        high = jnp.sum(jnp.where(lane < G, 0.0, part), axis=1, keepdims=True)
        coef_ref[k] = jnp.where(lane < G, low, high) / CELLS

    def one(i, carry):
        rows = pl.ds(pl.multiple_of(i * 64, 64), 64)
        same = jnp.zeros((64, 128), f32)
        cross = jnp.zeros((64, 128), f32)
        for o in range(COUPLES):
            phi = phi_ref[o, rows].astype(f32)
            same = same + phi * coef_ref[0, o : o + 1]
            cross = cross + phi * coef_ref[1, o : o + 1]
        out_ref[rows] = x_ref[rows] - same - pltpu.roll(cross, G, 1)
        return carry

    lax.fori_loop(0, 8, one, 0)


def vmem_specs(n):
    return [pl.BlockSpec(memory_space=pltpu.VMEM)] * n


def smem_specs(n):
    return [pl.BlockSpec(memory_space=pltpu.SMEM)] * n


def lane_exchange(mine, core):
    other = lax.ppermute(mine, "core", [(0, 1), (1, 0)])
    lane = lax.broadcasted_iota(jnp.int32, mine.shape, mine.ndim - 1)
    return jnp.where((lane < G) == (core == 0), mine, jnp.roll(other, G, axis=-1))


def moves():
    return [(z * NY + y, ((z & 1) * NY + y) * NY + (z >> 1)) for z in range(NZ) for y in range(NY)]


def local(orbitals, pair_table):
    z, x, y, core = (lax.axis_index(a) for a in ("z", "x", "y", "core"))
    mine = orbitals[0]
    live = pair_table[:, 0] >= 0
    code = jnp.where(live, pair_table[:, 0] + 32 * pair_table[:, 1] + 1024 * pair_table[:, 2], -1)
    codes = lax.all_gather(code[None], ("z", "x"), axis=0, tiled=True)
    own = lane_exchange(mine, core)
    left = lax.all_gather(lax.all_gather(own, "y", axis=0, tiled=True), "x", axis=0, tiled=True)
    right = lax.all_gather(lax.ppermute(own, ("z", "y"), moves()), "z", axis=0, tiled=True)
    right = lax.all_gather(right, "core", axis=0, tiled=True)
    phi_all = lax.all_gather(orbitals, ("z", "x"), axis=0, tiled=True)

    me = (z * 16 + x * 4 + y).astype(jnp.int32).reshape(1)
    tasks = pl.pallas_call(
        assign_kernel,
        out_shape=jax.ShapeDtypeStruct((17,), jnp.int32),
        in_specs=smem_specs(2),
        out_specs=pl.BlockSpec(memory_space=pltpu.SMEM),
        scratch_shapes=[pltpu.SMEM((NZ * NX * NY,), jnp.int32)],
        name="assign",
    )(me, codes)

    w_depth, w_rows, w_planes = (jnp.asarray(w) for w in weights())
    acc = jax.ShapeDtypeStruct((4, ROWS, 128), f32)
    lacc, racc = pl.pallas_call(
        pairs_kernel,
        out_shape=(acc, acc),
        in_specs=smem_specs(2) + vmem_specs(6),
        out_specs=tuple(vmem_specs(2)),
        scratch_shapes=[pltpu.VMEM((ROWS, 128), f32)],
        compiler_params=pltpu.CompilerParams(vmem_limit_bytes=48 * 1024 * 1024),
        name="pairs",
    )(
        core.astype(jnp.int32).reshape(1),
        tasks,
        left.reshape(4, ROWS, 128),
        right.reshape(4, ROWS, 128),
        w_depth,
        w_rows,
        w_planes,
        coulomb(),
    )

    from_left = lax.psum_scatter(lacc.reshape(NX, NY, 512, 128), "x", scatter_dimension=0, tiled=True)
    from_left = lax.psum_scatter(from_left[0], "y", scatter_dimension=0, tiled=True)
    from_right = lax.psum_scatter(racc.reshape(2, NZ, 512, 128), "core", scatter_dimension=0, tiled=True)
    from_right = lax.psum_scatter(from_right[0], "z", scatter_dimension=0, tiled=True)
    from_right = lax.ppermute(from_right, ("z", "y"), [(d, s) for s, d in moves()])
    action = lane_exchange((from_left + from_right)[0], core)

    phi_rows = phi_all.reshape(COUPLES, 512, 128)
    over = pl.pallas_call(
        overlap_kernel,
        out_shape=jax.ShapeDtypeStruct((COUPLES, 2, 128), f32),
        in_specs=vmem_specs(2),
        out_specs=vmem_specs(1)[0],
        scratch_shapes=[pltpu.VMEM((512, 128), f32)],
        name="overlap",
    )(action, phi_rows)
    over = lax.psum(over, ("y", "core"))
    out = pl.pallas_call(
        project_kernel,
        out_shape=jax.ShapeDtypeStruct((512, 128), f32),
        in_specs=vmem_specs(3),
        out_specs=vmem_specs(1)[0],
        scratch_shapes=[pltpu.VMEM((2, COUPLES, 128), f32)],
        name="project",
    )(action, phi_rows, over)
    return out.reshape(1, 8, G, 128)


def solution(mesh):
    grid = Mesh(mesh.devices.reshape(NZ, NX, NY, 2), ("z", "x", "y", "core"))
    placed = (P(("z", "x"), ("y", "core"), None, None), P(("z", "x"), None))
    return jax.shard_map(
        local,
        mesh=grid,
        in_specs=placed,
        out_specs=P(("z", "x"), ("y", "core"), None, None),
        check_vma=False,
    )
```

```python
import functools
import math

import jax
import jax.numpy as jnp
import ml_dtypes
import numpy as np
from jax import lax
from jax.experimental import pallas as pl
from jax.experimental.pallas import tpu as pltpu
from jax.sharding import Mesh
from jax.sharding import PartitionSpec as P

G = 64
ROWS = 2048
CHUNK = 256
KY_STEP = 4
NZ, NX, NY = 8, 4, 4
COUPLES = 32
CELLS = G * G * G
exchange_fraction = 0.25
cell_ratio = 8.0
f32, bf16 = jnp.float32, jnp.bfloat16


def split_np(mat):
    high = mat.astype(ml_dtypes.bfloat16)
    low = (mat - high.astype(np.float64)).astype(ml_dtypes.bfloat16)
    return high, low


def plane_order():
    r = np.arange(32)
    return [16 * (r // 8) + 8 * h + r % 8 for h in (0, 1)]


def weights():
    idx = np.arange(G)
    angles = 2.0 * np.pi / G * (idx[:, None] * idx[None, :] % G)
    hart = (np.cos(angles) + np.sin(angles)) / math.sqrt(G)
    high, low = split_np(np.kron(np.eye(2), hart))
    zero = np.zeros_like(high)
    w_depth = np.block([[high, low], [high, zero]])
    w_rows = np.block([[high, high], [low, zero]])
    s0, s1 = plane_order()
    mix = np.block(
        [
            [hart[np.ix_(s0, s0)], hart[np.ix_(s0, s1)]],
            [hart[np.ix_(s1, s1)], hart[np.ix_(s1, s0)]],
        ]
    )
    high, low = split_np(mix)
    w_planes = np.block([[high, high], [low, np.zeros_like(high)]])
    return w_depth, w_rows, w_planes


def coulomb():
    def folded(v):
        return jnp.minimum(v, G - v).astype(f32)

    lane = lax.broadcasted_iota(jnp.int32, (G, 32, 128), 2)
    row = lax.broadcasted_iota(jnp.int32, (G, 32, 128), 1)
    ky = folded(lax.broadcasted_iota(jnp.int32, (G, 32, 128), 0))
    kx = cell_ratio * folded(16 * (row // 8) + 8 * (lane // G) + row % 8)
    kz = folded(lane % G)
    scale = (2.0 * math.pi / G) * (2.0 * math.pi / G)
    squared = scale * (kx * kx + ky * ky + kz * kz)
    safe = jnp.where(squared > 0, squared, 1.0)
    return jnp.where(squared > 0, -exchange_fraction / safe, 0.0)


def assign_kernel(me_ref, code_ref, out_ref, load_ref):
    me = me_ref[0]

    def clear(i, carry):
        load_ref[i] = 0
        return carry

    lax.fori_loop(0, NZ * NX * NY, clear, 0)
    for i in range(17):
        out_ref[i] = 0

    def one_block(b, count):
        def live(state):
            s, _ = state
            return (s < 32) & (code_ref[b, jnp.minimum(s, 31)] >= 0)

        def step(state):
            s, cnt = state
            code = code_ref[b, s]
            m = code & 31
            n = (code >> 5) & 31
            flip = code >> 10
            mz, mx, nz, nx = m >> 2, m & 3, n >> 2, n & 3
            first = mz * 16 + nx * 4 + (nz >> 1)
            second = nz * 16 + mx * 4 + (mz >> 1)
            load_a = load_ref[first]
            load_b = load_ref[second]
            use_a = load_a <= load_b
            chip = jnp.where(use_a, first, second)
            load_ref[chip] = jnp.where(use_a, load_a, load_b) + 1
            task_a = mx + 4 * (nz & 1)
            task_b = nx + 4 * (mz & 1)
            task = jnp.where(use_a, task_a, task_b) + 8 * flip + 16 * (m == n).astype(jnp.int32)
            mine = chip == me

            @pl.when(mine)
            def _():
                out_ref[1 + cnt] = task

            return s + 1, cnt + mine.astype(jnp.int32)

        return lax.while_loop(live, step, (0, count))[1]

    out_ref[0] = lax.fori_loop(0, 32, one_block, 0)


def split(value):
    high = value.astype(bf16)
    return high, (value - high.astype(f32)).astype(bf16)


def depth_transform(value, w_depth):
    high, low = split(value)
    out = jnp.dot(jnp.concatenate([high, low], axis=1), w_depth, preferred_element_type=f32)
    return out[:, :128] + out[:, 128:]


def rows_transform(value, w_rows):
    high, low = split(value)
    half = CHUNK // 2
    top = jnp.concatenate([high[:half], high[half:]], axis=1)
    bottom = jnp.concatenate([low[:half], low[half:]], axis=1)
    out = jnp.dot(w_rows, jnp.concatenate([top, bottom], axis=0), preferred_element_type=f32)
    out = out[:half] + out[half:]
    return jnp.concatenate([out[:, :128], out[:, 128:]], axis=0)


def planes_transform(value, w_planes, low_lanes):
    turned = jnp.concatenate(
        [pltpu.roll(value[:, j * 128 : (j + 1) * 128], G, 1) for j in range(KY_STEP)], axis=1
    )
    vh, vl = split(value)
    th, tl = split(turned)
    out = jnp.dot(w_planes, jnp.concatenate([vh, th, vl, tl], axis=0), preferred_element_type=f32)
    out = out[:64] + out[64:]
    return jnp.where(low_lanes, out[:32], out[32:])


def pairs_kernel(
    tasks_ref, left_ref, same_ref, cross_ref, wz_ref, wy_ref, wx_ref, kern_ref, lacc_ref, sacc_ref, cacc_ref, t_ref
):
    def clear(i, carry):
        rows = pl.ds(pl.multiple_of(i * CHUNK, CHUNK), CHUNK)
        for k in range(4):
            lacc_ref[k, rows] = jnp.zeros((CHUNK, 128), f32)
        for k in range(2):
            sacc_ref[k, rows] = jnp.zeros((CHUNK, 128), f32)
            cacc_ref[k, rows] = jnp.zeros((CHUNK, 128), f32)
        return carry

    lax.fori_loop(0, ROWS // CHUNK, clear, 0)
    low_lanes = lax.broadcasted_iota(jnp.int32, (32, KY_STEP * 128), 1) % 128 < G

    def run(right_ref, racc_ref, task):
        a = task & 3
        b = (task >> 2) & 1
        second = 1.0 - (task >> 4).astype(f32)

        def forward(i, c):
            rows = pl.ds(pl.multiple_of(i * CHUNK, CHUNK), CHUNK)
            rho = left_ref[a, rows].astype(f32) * right_ref[b, rows].astype(f32)
            t_ref[rows] = rows_transform(depth_transform(rho, wz_ref[...]), wy_ref[...])
            return c

        lax.fori_loop(0, ROWS // CHUNK, forward, 0, unroll=2)

        def middle(i, c):
            first = i * KY_STEP
            value = jnp.concatenate(
                [t_ref[pl.ds(first + j, 32, stride=G)] for j in range(KY_STEP)], axis=1
            )
            kern = jnp.concatenate([kern_ref[first + j] for j in range(KY_STEP)], axis=1)
            value = planes_transform(value, wx_ref[...], low_lanes) * kern
            value = planes_transform(value, wx_ref[...], low_lanes)
            for j in range(KY_STEP):
                t_ref[pl.ds(first + j, 32, stride=G)] = value[:, j * 128 : (j + 1) * 128]
            return c

        lax.fori_loop(0, G // KY_STEP, middle, 0, unroll=2)

        def backward(i, c):
            rows = pl.ds(pl.multiple_of(i * CHUNK, CHUNK), CHUNK)
            v = depth_transform(rows_transform(t_ref[rows], wy_ref[...]), wz_ref[...])
            lacc_ref[a, rows] += v * right_ref[b, rows].astype(f32)
            racc_ref[b, rows] += (v * second) * left_ref[a, rows].astype(f32)
            return c

        lax.fori_loop(0, ROWS // CHUNK, backward, 0, unroll=2)

    def one_task(t, carry):
        task = tasks_ref[1 + t]
        flipped = (task >> 3) & 1 == 1

        @pl.when(jnp.logical_not(flipped))
        def _():
            run(same_ref, sacc_ref, task)

        @pl.when(flipped)
        def _():
            run(cross_ref, cacc_ref, task)

        return carry

    lax.fori_loop(0, tasks_ref[0], one_task, 0)


def overlap_kernel(x_ref, phi_ref, out_ref, turned_ref):
    for i in range(8):
        turned_ref[pl.ds(i * 64, 64)] = pltpu.roll(x_ref[pl.ds(i * 64, 64)], G, 1)

    def one(o, carry):
        same = jnp.zeros((64, 128), f32)
        cross = jnp.zeros((64, 128), f32)
        for i in range(8):
            rows = pl.ds(i * 64, 64)
            phi = phi_ref[o, rows].astype(f32)
            same = same + phi * x_ref[rows]
            cross = cross + phi * turned_ref[rows]
        out_ref[pl.ds(o, 1)] = jnp.sum(same, axis=0, keepdims=True)
        out_ref[pl.ds(COUPLES + o, 1)] = jnp.sum(cross, axis=0, keepdims=True)
        return carry

    lax.fori_loop(0, COUPLES, one, 0)


def project_kernel(x_ref, phi_ref, over_ref, out_ref, coef_ref):
    lane = lax.broadcasted_iota(jnp.int32, (COUPLES, 128), 1)
    for k in range(2):
        part = over_ref[pl.ds(k * COUPLES, COUPLES)]
        low = jnp.sum(jnp.where(lane < G, part, 0.0), axis=1, keepdims=True)
        high = jnp.sum(jnp.where(lane < G, 0.0, part), axis=1, keepdims=True)
        coef_ref[k] = jnp.where(lane < G, low, high) / CELLS

    def one(i, carry):
        rows = pl.ds(pl.multiple_of(i * 64, 64), 64)
        same = jnp.zeros((64, 128), f32)
        cross = jnp.zeros((64, 128), f32)
        for o in range(COUPLES):
            phi = phi_ref[o, rows].astype(f32)
            same = same + phi * coef_ref[0, o : o + 1]
            cross = cross + phi * coef_ref[1, o : o + 1]
        out_ref[rows] = x_ref[rows] - same - pltpu.roll(cross, G, 1)
        return carry

    lax.fori_loop(0, 8, one, 0)


def vmem_specs(n):
    return [pl.BlockSpec(memory_space=pltpu.VMEM)] * n


def smem_specs(n):
    return [pl.BlockSpec(memory_space=pltpu.SMEM)] * n


def lane_exchange(mine, core):
    other = lax.ppermute(mine, "core", [(0, 1), (1, 0)])
    lane = lax.broadcasted_iota(jnp.int32, mine.shape, mine.ndim - 1)
    return jnp.where((lane < G) == (core == 0), mine, jnp.roll(other, G, axis=-1))


def moves():
    return [(z * NY + y, ((z & 1) * NY + y) * NY + (z >> 1)) for z in range(NZ) for y in range(NY)]


def ring(size, step):
    return [(i, (i + step) % size) for i in range(size)]


def sum_over_slab(value):
    value = value + lax.ppermute(value, "core", ring(2, 1))
    near = lax.ppermute(value, "y", ring(NY, 1))
    back = lax.ppermute(value, "y", ring(NY, 3))
    far = lax.ppermute(value, "y", ring(NY, 2))
    return (value + far) + (near + back)


def local(orbitals, pair_table):
    z, x, y, core = (lax.axis_index(a) for a in ("z", "x", "y", "core"))
    mine = orbitals[0]
    live = pair_table[:, 0] >= 0
    code = jnp.where(live, pair_table[:, 0] + 32 * pair_table[:, 1] + 1024 * pair_table[:, 2], -1)
    codes = lax.all_gather(code[None], ("z", "x"), axis=0, tiled=True)
    phi_all = lax.all_gather(orbitals, ("z", "x"), axis=0, tiled=True)
    own = lane_exchange(mine, core)
    same = lax.all_gather(lax.ppermute(own, ("z", "y"), moves()), "z", axis=0, tiled=True)
    cross = lax.ppermute(same, "core", ring(2, 1))

    me = (z * 16 + x * 4 + y).astype(jnp.int32).reshape(1)
    tasks = pl.pallas_call(
        assign_kernel,
        out_shape=jax.ShapeDtypeStruct((17,), jnp.int32),
        in_specs=smem_specs(2),
        out_specs=pl.BlockSpec(memory_space=pltpu.SMEM),
        scratch_shapes=[pltpu.SMEM((NZ * NX * NY,), jnp.int32)],
        cost_estimate=pl.CostEstimate(flops=0, bytes_accessed=60 * 1000 * 1000, transcendentals=0),
        name="assign",
    )(me, codes)

    own, tasks = lax.optimization_barrier((own, tasks))
    spread = jnp.broadcast_to(own[None], (NX * NY,) + own.shape)
    left = lax.all_to_all(spread, ("x", "y"), split_axis=0, concat_axis=0, tiled=True)

    w_depth, w_rows, w_planes = (jnp.asarray(w) for w in weights())
    lacc, sacc, cacc = pl.pallas_call(
        pairs_kernel,
        out_shape=tuple(jax.ShapeDtypeStruct((k, ROWS, 128), f32) for k in (4, 2, 2)),
        in_specs=smem_specs(1) + vmem_specs(7),
        out_specs=tuple(vmem_specs(3)),
        scratch_shapes=[pltpu.VMEM((ROWS, 128), f32)],
        compiler_params=pltpu.CompilerParams(vmem_limit_bytes=48 * 1024 * 1024),
        cost_estimate=pl.CostEstimate(flops=0, bytes_accessed=180 * 1000 * 1000, transcendentals=0),
        name="pairs",
    )(
        tasks,
        left.reshape(4, ROWS, 128),
        same.reshape(2, ROWS, 128),
        cross.reshape(2, ROWS, 128),
        w_depth,
        w_rows,
        w_planes,
        coulomb(),
    )
    lacc, sacc, cacc, phi_all = lax.optimization_barrier((lacc, sacc, cacc, phi_all))

    racc = sacc + lax.ppermute(cacc, "core", ring(2, 1))
    lacc, racc = lax.optimization_barrier((lacc, racc))
    from_right = lax.psum_scatter(racc.reshape(NZ, 512, 128), "z", scatter_dimension=0, tiled=True)
    from_left = lax.all_to_all(
        lacc.reshape(NX * NY, 512, 128), ("x", "y"), split_axis=0, concat_axis=0, tiled=True
    )
    from_right = lax.ppermute(from_right[0], ("z", "y"), [(d, s) for s, d in moves()])
    action = lane_exchange(jnp.sum(from_left, axis=0) + from_right, core)

    phi_rows = phi_all.reshape(COUPLES, 512, 128)
    over = pl.pallas_call(
        overlap_kernel,
        out_shape=jax.ShapeDtypeStruct((2 * COUPLES, 128), f32),
        in_specs=vmem_specs(2),
        out_specs=vmem_specs(1)[0],
        scratch_shapes=[pltpu.VMEM((512, 128), f32)],
        name="overlap",
    )(action, phi_rows)
    out = pl.pallas_call(
        project_kernel,
        out_shape=jax.ShapeDtypeStruct((512, 128), f32),
        in_specs=vmem_specs(3),
        out_specs=vmem_specs(1)[0],
        scratch_shapes=[pltpu.VMEM((2, COUPLES, 128), f32)],
        name="project",
    )(action, phi_rows, sum_over_slab(over))
    return out.reshape(1, 8, G, 128)


def solution(mesh):
    grid = Mesh(mesh.devices.reshape(NZ, NX, NY, 2), ("z", "x", "y", "core"))
    placed = (P(("z", "x"), ("y", "core"), None, None), P(("z", "x"), None))
    return jax.shard_map(
        local,
        mesh=grid,
        in_specs=placed,
        out_specs=P(("z", "x"), ("y", "core"), None, None),
        check_vma=False,
    )
```

```python
import math

import jax
import jax.numpy as jnp
import ml_dtypes
import numpy as np
from jax import lax
from jax.experimental import pallas as pl
from jax.experimental.pallas import tpu as pltpu
from jax.sharding import Mesh
from jax.sharding import PartitionSpec as P

G = 64
ROWS = 2048
CHUNK = 256
KY_STEP = 32
NZ, NX, NY = 8, 4, 4
UNROLL = (8, 2, 8)
COUPLES = 32
CELLS = G * G * G
CODES = 64
FULL = 32500.0
exchange_fraction = 0.25
cell_ratio = 8.0
f32, bf16 = jnp.float32, jnp.bfloat16


def split_np(mat):
    high = mat.astype(ml_dtypes.bfloat16)
    low = (mat - high.astype(np.float64)).astype(ml_dtypes.bfloat16)
    return high, low


def plane_order():
    r = np.arange(32)
    return [16 * (r // 8) + 8 * h + r % 8 for h in (0, 1)]


def weights():
    idx = np.arange(G)
    angles = 2.0 * np.pi / G * (idx[:, None] * idx[None, :] % G)
    hart = (np.cos(angles) + np.sin(angles)) / math.sqrt(G)
    high, low = split_np(np.kron(np.eye(2), hart))
    zero = np.zeros_like(high)
    w_depth = np.block([[high, low], [high, zero]])
    w_rows = np.block([[high, high], [low, zero]])
    order = np.concatenate(plane_order())
    high, low = split_np(hart[np.ix_(order, order)])
    w_planes = np.block([[high, high], [low, np.zeros_like(high)]])
    return w_depth, w_rows, w_planes


def coulomb():
    def folded(v):
        return jnp.minimum(v, G - v).astype(f32)

    pair = lax.broadcasted_iota(jnp.int32, (G // 2, G, 128), 0)
    row = lax.broadcasted_iota(jnp.int32, (G // 2, G, 128), 1)
    lane = lax.broadcasted_iota(jnp.int32, (G // 2, G, 128), 2)
    ky = folded(2 * pair + lane // G)
    kx = cell_ratio * folded(16 * (row % 32 // 8) + 8 * (row // 32) + row % 8)
    kz = folded(lane % G)
    scale = (2.0 * math.pi / G) * (2.0 * math.pi / G)
    squared = scale * (kx * kx + ky * ky + kz * kz)
    safe = jnp.where(squared > 0, squared, 1.0)
    return jnp.where(squared > 0, -exchange_fraction / safe, 0.0)


def assign_kernel(me_ref, code_ref, out_ref, load_ref):
    me = me_ref[0]

    def clear(i, carry):
        load_ref[i] = 0
        return carry

    lax.fori_loop(0, NZ * NX * NY, clear, 0)
    for i in range(17):
        out_ref[i] = 0

    def one_block(b, count):
        def live(state):
            s, _ = state
            return (s < 32) & (code_ref[b, jnp.minimum(s, 31)] >= 0)

        def step(state):
            s, cnt = state
            code = code_ref[b, s]
            m = code & 31
            n = (code >> 5) & 31
            flip = code >> 10
            mz, mx, nz, nx = m >> 2, m & 3, n >> 2, n & 3
            first = mz * 16 + nx * 4 + (nz >> 1)
            second = nz * 16 + mx * 4 + (mz >> 1)
            load_a = load_ref[first]
            load_b = load_ref[second]
            use_a = load_a <= load_b
            chip = jnp.where(use_a, first, second)
            load_ref[chip] = jnp.where(use_a, load_a, load_b) + 1
            task_a = mx + 4 * (nz & 1)
            task_b = nx + 4 * (mz & 1)
            task = jnp.where(use_a, task_a, task_b) + 8 * flip + 16 * (m == n).astype(jnp.int32)
            mine = chip == me

            @pl.when(mine)
            def _():
                out_ref[1 + cnt] = task

            return s + 1, cnt + mine.astype(jnp.int32)

        return lax.while_loop(live, step, (0, count))[1]

    out_ref[0] = lax.fori_loop(0, 32, one_block, 0)


def split(value):
    high = value.astype(bf16)
    return high, (value - high.astype(f32)).astype(bf16)


def depth_transform(value, w_depth):
    high, low = split(value)
    out = jnp.dot(jnp.concatenate([high, low], axis=1), w_depth, preferred_element_type=f32)
    return out[:, :128] + out[:, 128:]


def rows_transform(value, w_rows):
    high, low = split(value)
    half = CHUNK // 2
    top = jnp.concatenate([high[:half], high[half:]], axis=1)
    bottom = jnp.concatenate([low[:half], low[half:]], axis=1)
    out = jnp.dot(w_rows, jnp.concatenate([top, bottom], axis=0), preferred_element_type=f32)
    out = out[:half] + out[half:]
    return jnp.concatenate([out[:, :128], out[:, 128:]], axis=0)


def planes_transform(value, w_planes):
    high, low = split(value)
    out = jnp.dot(w_planes, jnp.concatenate([high, low], axis=0), preferred_element_type=f32)
    return out[:G] + out[G:]


def gather_planes(t_ref, first, low_lanes):
    tops, bottoms = [], []
    for base in range(0, KY_STEP, 8):
        block = jnp.concatenate(
            [t_ref[pl.ds(pl.multiple_of(r * G + first + base, 8), 8)][None] for r in range(32)], axis=0
        )
        block = jnp.swapaxes(block, 0, 1)
        for p in range(0, 8, 2):
            tops.append(jnp.where(low_lanes, block[p], pltpu.roll(block[p + 1], G, 1)))
            bottoms.append(jnp.where(low_lanes, pltpu.roll(block[p], G, 1), block[p + 1]))
    return jnp.concatenate([jnp.concatenate(tops, axis=1), jnp.concatenate(bottoms, axis=1)], axis=0)


def scatter_planes(t_ref, first, value, low_lanes):
    for base in range(0, KY_STEP, 8):
        rows = []
        for p in range(base // 2, base // 2 + 4):
            top = value[:32, p * 128 : (p + 1) * 128]
            bottom = value[32:, p * 128 : (p + 1) * 128]
            rows.append(jnp.where(low_lanes, top, pltpu.roll(bottom, G, 1))[None])
            rows.append(jnp.where(low_lanes, pltpu.roll(top, G, 1), bottom)[None])
        block = jnp.swapaxes(jnp.concatenate(rows, axis=0), 0, 1)
        for r in range(32):
            t_ref[pl.ds(pl.multiple_of(r * G + first + base, 8), 8)] = block[r]


def pairs_kernel(
    tasks_ref, left_ref, same_ref, cross_ref, wz_ref, wy_ref, wx_ref, kern_ref, lacc_ref, sacc_ref, cacc_ref, t_ref
):
    def clear(i, carry):
        rows = pl.ds(pl.multiple_of(i * CHUNK, CHUNK), CHUNK)
        for k in range(4):
            lacc_ref[k, rows] = jnp.zeros((CHUNK, 128), f32)
        for k in range(2):
            sacc_ref[k, rows] = jnp.zeros((CHUNK, 128), f32)
            cacc_ref[k, rows] = jnp.zeros((CHUNK, 128), f32)
        return carry

    lax.fori_loop(0, ROWS // CHUNK, clear, 0)
    low_lanes = lax.broadcasted_iota(jnp.int32, (32, 128), 1) < G

    def run(right_ref, racc_ref, task):
        a = task & 3
        b = (task >> 2) & 1
        second = 1.0 - (task >> 4).astype(f32)

        def forward(i, c):
            rows = pl.ds(pl.multiple_of(i * CHUNK, CHUNK), CHUNK)
            rho = left_ref[a, rows].astype(f32) * right_ref[b, rows].astype(f32)
            t_ref[rows] = rows_transform(depth_transform(rho, wz_ref[...]), wy_ref[...])
            return c

        lax.fori_loop(0, ROWS // CHUNK, forward, 0, unroll=UNROLL[0])

        def middle(i, c):
            first = pl.multiple_of(i * KY_STEP, KY_STEP)
            value = gather_planes(t_ref, first, low_lanes)
            kern = jnp.concatenate(
                [kern_ref[i * (KY_STEP // 2) + j] for j in range(KY_STEP // 2)], axis=1
            )
            value = planes_transform(value, wx_ref[...]) * kern
            value = planes_transform(value, wx_ref[...])
            scatter_planes(t_ref, first, value, low_lanes)
            return c

        lax.fori_loop(0, G // KY_STEP, middle, 0, unroll=UNROLL[1])

        def backward(i, c):
            rows = pl.ds(pl.multiple_of(i * CHUNK, CHUNK), CHUNK)
            v = depth_transform(rows_transform(t_ref[rows], wy_ref[...]), wz_ref[...])
            lacc_ref[a, rows] += v * right_ref[b, rows].astype(f32)
            racc_ref[b, rows] += (v * second) * left_ref[a, rows].astype(f32)
            return c

        lax.fori_loop(0, ROWS // CHUNK, backward, 0, unroll=UNROLL[2])

    def one_task(t, carry):
        task = tasks_ref[1 + t]
        flipped = (task >> 3) & 1 == 1

        @pl.when(jnp.logical_not(flipped))
        def _():
            run(same_ref, sacc_ref, task)

        @pl.when(flipped)
        def _():
            run(cross_ref, cacc_ref, task)

        return carry

    lax.fori_loop(0, tasks_ref[0], one_task, 0)


def quantize_piece(value_of, write):
    codes = []
    for p in range(8):
        rows = pl.ds(p * G, G)
        value = value_of(rows)
        largest = jnp.max(jnp.abs(value), axis=0, keepdims=True)
        code = jnp.ceil(jnp.log2(jnp.maximum(largest, 1e-30)) * CODES)
        codes.append(code)
        value = jnp.round(value * (jnp.exp2(code * (-1.0 / CODES)) * FULL))
        write(rows, value.astype(jnp.int32).astype(jnp.int16))
    codes = jnp.concatenate(codes + [jnp.zeros((8, 128), f32)], axis=0)
    write(pl.ds(512, 16), codes.astype(jnp.int32).astype(jnp.int16))


def quantize_left_kernel(in_ref, out_ref):
    for k in range(out_ref.shape[0]):

        def write(rows, value):
            out_ref[k, rows] = value

        quantize_piece(lambda rows: in_ref[k, rows], write)


def quantize_right_kernel(z_ref, first_ref, second_ref, *out_refs):
    for k in range(NZ):
        piece = (z_ref[0] + k) & (NZ - 1)

        def write(rows, value):
            out_refs[k][rows] = value

        quantize_piece(lambda rows: first_ref[piece, rows] + second_ref[piece, rows], write)


def combine_kernel(left_ref, *refs):
    out_ref = refs[-1]

    def read(part, rows):
        ref = left_ref.at[part] if part < NX * NY else refs[part - NX * NY]
        return ref[rows].astype(jnp.int32).astype(f32)

    count = NX * NY + NZ
    scales = [
        jnp.exp2(read(k, pl.ds(512, 16))[:8] * (1.0 / CODES)) * (1.0 / FULL) for k in range(count)
    ]
    for p in range(8):
        rows = pl.ds(p * G, G)
        total = jnp.zeros((G, 128), f32)
        for k in range(count):
            total = total + read(k, rows) * scales[k][p : p + 1]
        out_ref[rows] = total


def quantize_left(lacc):
    pieces, step = NX * NY, 4
    return pl.pallas_call(
        quantize_left_kernel,
        grid=(pieces // step,),
        out_shape=jax.ShapeDtypeStruct((pieces, 528, 128), jnp.int16),
        in_specs=[pl.BlockSpec((step, 512, 128), lambda i: (i, 0, 0))],
        out_specs=pl.BlockSpec((step, 528, 128), lambda i: (i, 0, 0)),
        cost_estimate=pl.CostEstimate(flops=0, bytes_accessed=10 * 1000 * 1000, transcendentals=0),
        name="quantize_left",
    )(lacc)


def quantize_right(z, first, second):
    return pl.pallas_call(
        quantize_right_kernel,
        out_shape=(jax.ShapeDtypeStruct((528, 128), jnp.int16),) * NZ,
        in_specs=smem_specs(1) + vmem_specs(2),
        out_specs=tuple(vmem_specs(NZ)),
        cost_estimate=pl.CostEstimate(flops=0, bytes_accessed=8 * 1000 * 1000, transcendentals=0),
        name="quantize_right",
    )(z.astype(jnp.int32).reshape(1), first, second)


def combine(left_parts, right_parts):
    return pl.pallas_call(
        combine_kernel,
        out_shape=jax.ShapeDtypeStruct((512, 128), f32),
        in_specs=vmem_specs(1 + len(right_parts)),
        out_specs=vmem_specs(1)[0],
        name="combine",
    )(left_parts, *right_parts)


def overlap_kernel(core_ref, own_ref, other_ref, phi_ref, x_ref, out_ref, same_ref, cross_ref):
    keep = (lax.broadcasted_iota(jnp.int32, (G, 128), 1) < G) == (core_ref[0] == 0)
    same_ref[...] = jnp.zeros_like(same_ref)
    cross_ref[...] = jnp.zeros_like(cross_ref)

    def rows_block(i, carry):
        rows = pl.ds(pl.multiple_of(i * G, G), G)
        value = jnp.where(keep, own_ref[rows], pltpu.roll(other_ref[rows], G, 1))
        turned = pltpu.roll(value, G, 1)
        x_ref[rows] = value
        for o in range(COUPLES):
            phi = phi_ref[o, rows].astype(f32)
            same_ref[o] += jnp.sum((phi * value).reshape(8, 8, 128), axis=0)
            cross_ref[o] += jnp.sum((phi * turned).reshape(8, 8, 128), axis=0)
        return carry

    lax.fori_loop(0, 8, rows_block, 0)
    out_ref[pl.ds(0, COUPLES)] = jnp.sum(same_ref[...], axis=1)
    out_ref[pl.ds(COUPLES, COUPLES)] = jnp.sum(cross_ref[...], axis=1)


def project_kernel(x_ref, phi_ref, over_ref, out_ref, coef_ref):
    lane = lax.broadcasted_iota(jnp.int32, (COUPLES, 128), 1)
    for k in range(2):
        part = over_ref[pl.ds(k * COUPLES, COUPLES)]
        low = jnp.sum(jnp.where(lane < G, part, 0.0), axis=1, keepdims=True)
        high = jnp.sum(jnp.where(lane < G, 0.0, part), axis=1, keepdims=True)
        coef_ref[k] = jnp.where(lane < G, low, high) / CELLS

    def rows_block(i, carry):
        rows = pl.ds(pl.multiple_of(i * G, G), G)
        same = jnp.zeros((G, 128), f32)
        cross = jnp.zeros((G, 128), f32)
        for o in range(COUPLES):
            phi = phi_ref[o, rows].astype(f32)
            same = same + phi * coef_ref[0, o : o + 1]
            cross = cross + phi * coef_ref[1, o : o + 1]
        out_ref[rows] = x_ref[rows] - same - pltpu.roll(cross, G, 1)
        return carry

    lax.fori_loop(0, 8, rows_block, 0)


def vmem_specs(n):
    return [pl.BlockSpec(memory_space=pltpu.VMEM)] * n


def smem_specs(n):
    return [pl.BlockSpec(memory_space=pltpu.SMEM)] * n


def lane_exchange(mine, core):
    other = lax.ppermute(mine, "core", [(0, 1), (1, 0)])
    lane = lax.broadcasted_iota(jnp.int32, mine.shape, mine.ndim - 1)
    return jnp.where((lane < G) == (core == 0), mine, jnp.roll(other, G, axis=-1))


def moves():
    return [(z * NY + y, ((z & 1) * NY + y) * NY + (z >> 1)) for z in range(NZ) for y in range(NY)]


def ring(size, step):
    return [(i, (i + step) % size) for i in range(size)]


def sum_over_slab(value):
    value = value + lax.ppermute(value, "core", ring(2, 1))
    near = lax.ppermute(value, "y", ring(NY, 1))
    back = lax.ppermute(value, "y", ring(NY, 3))
    far = lax.ppermute(value, "y", ring(NY, 2))
    return (value + far) + (near + back)


def returns(k):
    pairs = []
    for z in range(NZ):
        for y in range(NY):
            q = (z + k) % NZ
            pairs.append((z * NY + y, (2 * y + q // NY) * NY + q % NY))
    return pairs


def local(orbitals, pair_table):
    z, x, y, core = (lax.axis_index(a) for a in ("z", "x", "y", "core"))
    mine = orbitals[0]
    live = pair_table[:, 0] >= 0
    code = jnp.where(live, pair_table[:, 0] + 32 * pair_table[:, 1] + 1024 * pair_table[:, 2], -1)
    own = lane_exchange(mine, core)
    phi_all = lax.all_gather(orbitals, ("z", "x"), axis=0, tiled=True)
    moved = lax.ppermute(own, ("z", "y"), moves())
    own, code = lax.optimization_barrier((own, code))
    codes = lax.all_gather(code[None], ("z", "x"), axis=0, tiled=True)
    moved, own, codes = lax.optimization_barrier((moved, own, codes))
    same = lax.all_gather(moved, "z", axis=0, tiled=True)
    spread = jnp.broadcast_to(own[None], (NX * NY,) + own.shape)
    left = lax.all_to_all(spread, ("x", "y"), split_axis=0, concat_axis=0, tiled=True)

    me = (z * 16 + x * 4 + y).astype(jnp.int32).reshape(1)
    tasks = pl.pallas_call(
        assign_kernel,
        out_shape=jax.ShapeDtypeStruct((17,), jnp.int32),
        in_specs=smem_specs(2),
        out_specs=pl.BlockSpec(memory_space=pltpu.SMEM),
        scratch_shapes=[pltpu.SMEM((NZ * NX * NY,), jnp.int32)],
        cost_estimate=pl.CostEstimate(flops=0, bytes_accessed=60 * 1000 * 1000, transcendentals=0),
        name="assign",
    )(me, codes)
    same, tasks = lax.optimization_barrier((same, tasks))
    cross = lax.ppermute(same, "core", ring(2, 1))

    w_depth, w_rows, w_planes = (jnp.asarray(w) for w in weights())
    lacc, sacc, cacc = pl.pallas_call(
        pairs_kernel,
        out_shape=tuple(jax.ShapeDtypeStruct((k, ROWS, 128), f32) for k in (4, 2, 2)),
        in_specs=smem_specs(1) + vmem_specs(7),
        out_specs=tuple(vmem_specs(3)),
        scratch_shapes=[pltpu.VMEM((ROWS, 128), f32)],
        compiler_params=pltpu.CompilerParams(vmem_limit_bytes=48 * 1024 * 1024),
        cost_estimate=pl.CostEstimate(flops=0, bytes_accessed=180 * 1000 * 1000, transcendentals=0),
        name="pairs",
    )(
        tasks,
        left.reshape(4, ROWS, 128),
        same.reshape(2, ROWS, 128),
        cross.reshape(2, ROWS, 128),
        w_depth,
        w_rows,
        w_planes,
        coulomb(),
    )
    lacc, sacc, cacc, phi_all = lax.optimization_barrier((lacc, sacc, cacc, phi_all))

    other = lax.ppermute(cacc, "core", ring(2, 1))
    right_parts = quantize_right(z, sacc.reshape(NZ, 512, 128), other.reshape(NZ, 512, 128))
    left_parts = quantize_left(lacc.reshape(NX * NY, 512, 128))
    left_parts, *right_parts = lax.optimization_barrier((left_parts, *right_parts))
    left_parts = lax.all_to_all(left_parts, ("x", "y"), split_axis=0, concat_axis=0, tiled=True)
    right_parts = [
        lax.ppermute(part, ("z", "y"), returns(k)) for k, part in enumerate(right_parts)
    ]
    action = combine(left_parts, right_parts)
    action_other = lax.ppermute(action, "core", ring(2, 1))

    phi_rows = phi_all.reshape(COUPLES, 512, 128)
    slab_action, over = pl.pallas_call(
        overlap_kernel,
        out_shape=(
            jax.ShapeDtypeStruct((512, 128), f32),
            jax.ShapeDtypeStruct((2 * COUPLES, 128), f32),
        ),
        in_specs=smem_specs(1) + vmem_specs(3),
        out_specs=tuple(vmem_specs(2)),
        scratch_shapes=[pltpu.VMEM((COUPLES, 8, 128), f32)] * 2,
        name="overlap",
    )(core.astype(jnp.int32).reshape(1), action, action_other, phi_rows)
    out = pl.pallas_call(
        project_kernel,
        out_shape=jax.ShapeDtypeStruct((512, 128), f32),
        in_specs=vmem_specs(3),
        out_specs=vmem_specs(1)[0],
        scratch_shapes=[pltpu.VMEM((2, COUPLES, 128), f32)],
        name="project",
    )(slab_action, phi_rows, sum_over_slab(over))
    return out.reshape(1, 8, G, 128)


def solution(mesh):
    grid = Mesh(mesh.devices.reshape(NZ, NX, NY, 2), ("z", "x", "y", "core"))
    placed = (P(("z", "x"), ("y", "core"), None, None), P(("z", "x"), None))
    return jax.shard_map(
        local,
        mesh=grid,
        in_specs=placed,
        out_specs=P(("z", "x"), ("y", "core"), None, None),
        check_vma=False,
    )
```

```python
import math

import jax
import jax.numpy as jnp
import ml_dtypes
import numpy as np
from jax import lax
from jax.experimental import pallas as pl
from jax.experimental.pallas import tpu as pltpu
from jax.sharding import Mesh
from jax.sharding import PartitionSpec as P

G = 64
ROWS = 2048
CHUNK = 256
KY_STEP = 32
NZ, NX, NY = 8, 4, 4
UNROLL = (8, 2, 8)
COUPLES = 32
CELLS = G * G * G
CODES = 64
FULL = 32500.0
exchange_fraction = 0.25
cell_ratio = 8.0
f32, bf16 = jnp.float32, jnp.bfloat16


def split_np(mat):
    high = mat.astype(ml_dtypes.bfloat16)
    low = (mat - high.astype(np.float64)).astype(ml_dtypes.bfloat16)
    return high, low


def plane_order():
    r = np.arange(32)
    return [16 * (r // 8) + 8 * h + r % 8 for h in (0, 1)]


def weights():
    idx = np.arange(G)
    angles = 2.0 * np.pi / G * (idx[:, None] * idx[None, :] % G)
    hart = (np.cos(angles) + np.sin(angles)) / math.sqrt(G)
    high, low = split_np(np.kron(np.eye(2), hart))
    zero = np.zeros_like(high)
    w_depth = np.block([[high, low], [high, zero]])
    w_rows = np.block([[high, high], [low, zero]])
    order = np.concatenate(plane_order())
    high, low = split_np(hart[np.ix_(order, order)])
    w_planes = np.block([[high, high], [low, np.zeros_like(high)]])
    return w_depth, w_rows, w_planes


def coulomb():
    def folded(v):
        return jnp.minimum(v, G - v).astype(f32)

    pair = lax.broadcasted_iota(jnp.int32, (G // 2, G, 128), 0)
    row = lax.broadcasted_iota(jnp.int32, (G // 2, G, 128), 1)
    lane = lax.broadcasted_iota(jnp.int32, (G // 2, G, 128), 2)
    ky = folded(2 * pair + lane // G)
    kx = cell_ratio * folded(16 * (row % 32 // 8) + 8 * (row // 32) + row % 8)
    kz = folded(lane % G)
    scale = (2.0 * math.pi / G) * (2.0 * math.pi / G)
    squared = scale * (kx * kx + ky * ky + kz * kz)
    safe = jnp.where(squared > 0, squared, 1.0)
    return jnp.where(squared > 0, -exchange_fraction / safe, 0.0)


def assign_kernel(me_ref, code_ref, out_ref, load_ref):
    me = me_ref[0]

    def clear(i, carry):
        load_ref[i] = 0
        return carry

    lax.fori_loop(0, NZ * NX * NY, clear, 0)
    for i in range(17):
        out_ref[i] = 0

    def one_block(b, count):
        def live(state):
            s, _ = state
            return (s < 32) & (code_ref[b, jnp.minimum(s, 31)] >= 0)

        def step(state):
            s, cnt = state
            code = code_ref[b, s]
            m = code & 31
            n = (code >> 5) & 31
            flip = code >> 10
            mz, mx, nz, nx = m >> 2, m & 3, n >> 2, n & 3
            first = mz * 16 + nx * 4 + (nz >> 1)
            second = nz * 16 + mx * 4 + (mz >> 1)
            load_a = load_ref[first]
            load_b = load_ref[second]
            use_a = load_a <= load_b
            chip = jnp.where(use_a, first, second)
            load_ref[chip] = jnp.where(use_a, load_a, load_b) + 1
            task_a = mx + 4 * (nz & 1)
            task_b = nx + 4 * (mz & 1)
            task = jnp.where(use_a, task_a, task_b) + 8 * flip + 16 * (m == n).astype(jnp.int32)
            mine = chip == me

            @pl.when(mine)
            def _():
                out_ref[1 + cnt] = task

            return s + 1, cnt + mine.astype(jnp.int32)

        return lax.while_loop(live, step, (0, count))[1]

    out_ref[0] = lax.fori_loop(0, 32, one_block, 0)


def split(value):
    high = value.astype(bf16)
    return high, (value - high.astype(f32)).astype(bf16)


def depth_transform(value, w_depth):
    high, low = split(value)
    out = jnp.dot(jnp.concatenate([high, low], axis=1), w_depth, preferred_element_type=f32)
    return out[:, :128] + out[:, 128:]


def rows_transform(value, w_rows):
    high, low = split(value)
    half = CHUNK // 2
    top = jnp.concatenate([high[:half], high[half:]], axis=1)
    bottom = jnp.concatenate([low[:half], low[half:]], axis=1)
    out = jnp.dot(w_rows, jnp.concatenate([top, bottom], axis=0), preferred_element_type=f32)
    out = out[:half] + out[half:]
    return jnp.concatenate([out[:, :128], out[:, 128:]], axis=0)


def planes_transform(value, w_planes):
    high, low = split(value)
    out = jnp.dot(w_planes, jnp.concatenate([high, low], axis=0), preferred_element_type=f32)
    return out[:G] + out[G:]


def gather_planes(t_ref, first, low_lanes):
    tops, bottoms = [], []
    for base in range(0, KY_STEP, 8):
        block = jnp.concatenate(
            [t_ref[pl.ds(pl.multiple_of(r * G + first + base, 8), 8)][None] for r in range(32)], axis=0
        )
        block = jnp.swapaxes(block, 0, 1)
        for p in range(0, 8, 2):
            tops.append(jnp.where(low_lanes, block[p], pltpu.roll(block[p + 1], G, 1)))
            bottoms.append(jnp.where(low_lanes, pltpu.roll(block[p], G, 1), block[p + 1]))
    return jnp.concatenate([jnp.concatenate(tops, axis=1), jnp.concatenate(bottoms, axis=1)], axis=0)


def scatter_planes(t_ref, first, value, low_lanes):
    for base in range(0, KY_STEP, 8):
        rows = []
        for p in range(base // 2, base // 2 + 4):
            top = value[:32, p * 128 : (p + 1) * 128]
            bottom = value[32:, p * 128 : (p + 1) * 128]
            rows.append(jnp.where(low_lanes, top, pltpu.roll(bottom, G, 1))[None])
            rows.append(jnp.where(low_lanes, pltpu.roll(top, G, 1), bottom)[None])
        block = jnp.swapaxes(jnp.concatenate(rows, axis=0), 0, 1)
        for r in range(32):
            t_ref[pl.ds(pl.multiple_of(r * G + first + base, 8), 8)] = block[r]


def pairs_kernel(
    core_ref,
    tasks_ref,
    left_ref,
    mine_ref,
    other_ref,
    wz_ref,
    wy_ref,
    wx_ref,
    kern_ref,
    lacc_ref,
    sacc_ref,
    cacc_ref,
    t_ref,
    same_ref,
    cross_ref,
):
    def clear(i, carry):
        rows = pl.ds(pl.multiple_of(i * CHUNK, CHUNK), CHUNK)
        for k in range(4):
            lacc_ref[k, rows] = jnp.zeros((CHUNK, 128), f32)
        for k in range(2):
            sacc_ref[k, rows] = jnp.zeros((CHUNK, 128), f32)
            cacc_ref[k, rows] = jnp.zeros((CHUNK, 128), f32)
        return carry

    lax.fori_loop(0, ROWS // CHUNK, clear, 0)
    keep = (lax.broadcasted_iota(jnp.int32, (G, 128), 1) < G) == (core_ref[0] == 0)

    def exchange(i, carry):
        source = pl.ds(pl.multiple_of(i * G, G), G)
        for j in range(8):
            mine = mine_ref[j, source].astype(f32)
            other = other_ref[j, source].astype(f32)
            rows = pl.ds(pl.multiple_of((j // 2) * 512 + i * G, G), G)
            same_ref[j % 2, rows] = jnp.where(keep, mine, pltpu.roll(other, G, 1)).astype(bf16)
            cross_ref[j % 2, rows] = jnp.where(keep, pltpu.roll(mine, G, 1), other).astype(bf16)
        return carry

    lax.fori_loop(0, 8, exchange, 0)
    low_lanes = lax.broadcasted_iota(jnp.int32, (32, 128), 1) < G

    def run(right_ref, racc_ref, task):
        a = task & 3
        b = (task >> 2) & 1
        second = 1.0 - (task >> 4).astype(f32)

        def forward(i, c):
            rows = pl.ds(pl.multiple_of(i * CHUNK, CHUNK), CHUNK)
            rho = left_ref[a, rows].astype(f32) * right_ref[b, rows].astype(f32)
            t_ref[rows] = rows_transform(depth_transform(rho, wz_ref[...]), wy_ref[...])
            return c

        lax.fori_loop(0, ROWS // CHUNK, forward, 0, unroll=UNROLL[0])

        def middle(i, c):
            first = pl.multiple_of(i * KY_STEP, KY_STEP)
            value = gather_planes(t_ref, first, low_lanes)
            kern = jnp.concatenate(
                [kern_ref[i * (KY_STEP // 2) + j] for j in range(KY_STEP // 2)], axis=1
            )
            value = planes_transform(value, wx_ref[...]) * kern
            value = planes_transform(value, wx_ref[...])
            scatter_planes(t_ref, first, value, low_lanes)
            return c

        lax.fori_loop(0, G // KY_STEP, middle, 0, unroll=UNROLL[1])

        def backward(i, c):
            rows = pl.ds(pl.multiple_of(i * CHUNK, CHUNK), CHUNK)
            v = depth_transform(rows_transform(t_ref[rows], wy_ref[...]), wz_ref[...])
            lacc_ref[a, rows] += v * right_ref[b, rows].astype(f32)
            racc_ref[b, rows] += (v * second) * left_ref[a, rows].astype(f32)
            return c

        lax.fori_loop(0, ROWS // CHUNK, backward, 0, unroll=UNROLL[2])

    def one_task(t, carry):
        task = tasks_ref[1 + t]
        flipped = (task >> 3) & 1 == 1

        @pl.when(jnp.logical_not(flipped))
        def _():
            run(same_ref, sacc_ref, task)

        @pl.when(flipped)
        def _():
            run(cross_ref, cacc_ref, task)

        return carry

    lax.fori_loop(0, tasks_ref[0], one_task, 0)


def quantize_piece(value_of, write):
    codes = []
    for p in range(8):
        rows = pl.ds(p * G, G)
        value = value_of(p)
        largest = jnp.max(jnp.abs(value), axis=0, keepdims=True)
        code = jnp.ceil(jnp.log2(jnp.maximum(largest, 1e-30)) * CODES)
        codes.append(code)
        value = jnp.round(value * (jnp.exp2(code * (-1.0 / CODES)) * FULL))
        write(rows, value.astype(jnp.int32).astype(jnp.int16))
    codes = jnp.concatenate(codes + [jnp.zeros((8, 128), f32)], axis=0)
    write(pl.ds(512, 16), codes.astype(jnp.int32).astype(jnp.int16))


def quantize_left_kernel(in_ref, out_ref):
    for k in range(out_ref.shape[0]):

        def write(rows, value):
            out_ref[k, rows] = value

        quantize_piece(lambda p: in_ref[k, pl.ds(p * G, G)], write)


def quantize_right_kernel(z_ref, first_ref, second_ref, *out_refs):
    for k in range(NZ):
        piece = (z_ref[0] + k) & (NZ - 1)

        def write(rows, value):
            out_refs[k][rows] = value

        def value_of(p):
            rows = pl.ds(p * G, G)
            return first_ref[piece, rows] + second_ref[piece, rows]

        quantize_piece(value_of, write)


def piece_sum(parts):
    def read(part, rows):
        return part[rows].astype(jnp.int32).astype(f32)

    scales = [jnp.exp2(read(part, pl.ds(512, 16))[:8] * (1.0 / CODES)) * (1.0 / FULL) for part in parts]

    def value_of(p):
        total = jnp.zeros((G, 128), f32)
        for part, scale in zip(parts, scales):
            total = total + read(part, pl.ds(p * G, G)) * scale[p : p + 1]
        return total

    return value_of


def combine_kernel(left_ref, right_ref, out_ref):
    value_of = piece_sum([left_ref.at[k] for k in range(NX * NY)] + [right_ref])
    for p in range(8):
        out_ref[pl.ds(p * G, G)] = value_of(p)


def combine_right_kernel(*refs):
    value_of = piece_sum(refs[:-1])

    def write(rows, value):
        refs[-1][rows] = value

    quantize_piece(value_of, write)


def quantize_left(lacc):
    pieces, step = NX * NY, 4
    return pl.pallas_call(
        quantize_left_kernel,
        grid=(pieces // step,),
        out_shape=jax.ShapeDtypeStruct((pieces, 528, 128), jnp.int16),
        in_specs=[pl.BlockSpec((step, 512, 128), lambda i: (i, 0, 0))],
        out_specs=pl.BlockSpec((step, 528, 128), lambda i: (i, 0, 0)),
        cost_estimate=pl.CostEstimate(flops=0, bytes_accessed=10 * 1000 * 1000, transcendentals=0),
        name="quantize_left",
    )(lacc)


def quantize_right(z, first, second):
    return pl.pallas_call(
        quantize_right_kernel,
        out_shape=(jax.ShapeDtypeStruct((528, 128), jnp.int16),) * NZ,
        in_specs=smem_specs(1) + vmem_specs(2),
        out_specs=tuple(vmem_specs(NZ)),
        cost_estimate=pl.CostEstimate(flops=0, bytes_accessed=8 * 1000 * 1000, transcendentals=0),
        name="quantize_right",
    )(z.astype(jnp.int32).reshape(1), first, second)


def combine(left_parts, right_part):
    return pl.pallas_call(
        combine_kernel,
        out_shape=jax.ShapeDtypeStruct((512, 128), f32),
        in_specs=vmem_specs(2),
        out_specs=vmem_specs(1)[0],
        name="combine",
    )(left_parts, right_part)


def combine_right(parts):
    return pl.pallas_call(
        combine_right_kernel,
        out_shape=jax.ShapeDtypeStruct((528, 128), jnp.int16),
        in_specs=vmem_specs(len(parts)),
        out_specs=vmem_specs(1)[0],
        cost_estimate=pl.CostEstimate(flops=0, bytes_accessed=6 * 1000 * 1000, transcendentals=0),
        name="combine_right",
    )(*parts)


def overlap_kernel(core_ref, own_ref, other_ref, phi_ref, x_ref, out_ref, same_ref, cross_ref):
    keep = (lax.broadcasted_iota(jnp.int32, (G, 128), 1) < G) == (core_ref[0] == 0)
    same_ref[...] = jnp.zeros_like(same_ref)
    cross_ref[...] = jnp.zeros_like(cross_ref)

    def rows_block(i, carry):
        rows = pl.ds(pl.multiple_of(i * G, G), G)
        value = jnp.where(keep, own_ref[rows], pltpu.roll(other_ref[rows], G, 1))
        turned = pltpu.roll(value, G, 1)
        x_ref[rows] = value
        for o in range(COUPLES):
            phi = phi_ref[o, rows].astype(f32)
            same_ref[o] += jnp.sum((phi * value).reshape(8, 8, 128), axis=0)
            cross_ref[o] += jnp.sum((phi * turned).reshape(8, 8, 128), axis=0)
        return carry

    lax.fori_loop(0, 8, rows_block, 0)
    out_ref[pl.ds(0, COUPLES)] = jnp.sum(same_ref[...], axis=1)
    out_ref[pl.ds(COUPLES, COUPLES)] = jnp.sum(cross_ref[...], axis=1)


def project_kernel(x_ref, phi_ref, over_ref, out_ref, coef_ref):
    lane = lax.broadcasted_iota(jnp.int32, (COUPLES, 128), 1)
    for k in range(2):
        part = over_ref[pl.ds(k * COUPLES, COUPLES)]
        low = jnp.sum(jnp.where(lane < G, part, 0.0), axis=1, keepdims=True)
        high = jnp.sum(jnp.where(lane < G, 0.0, part), axis=1, keepdims=True)
        coef_ref[k] = jnp.where(lane < G, low, high) / CELLS

    def rows_block(i, carry):
        rows = pl.ds(pl.multiple_of(i * G, G), G)
        same = jnp.zeros((G, 128), f32)
        cross = jnp.zeros((G, 128), f32)
        for o in range(COUPLES):
            phi = phi_ref[o, rows].astype(f32)
            same = same + phi * coef_ref[0, o : o + 1]
            cross = cross + phi * coef_ref[1, o : o + 1]
        out_ref[rows] = x_ref[rows] - same - pltpu.roll(cross, G, 1)
        return carry

    lax.fori_loop(0, 8, rows_block, 0)


def vmem_specs(n):
    return [pl.BlockSpec(memory_space=pltpu.VMEM)] * n


def smem_specs(n):
    return [pl.BlockSpec(memory_space=pltpu.SMEM)] * n


def lane_exchange(mine, core):
    other = lax.ppermute(mine, "core", [(0, 1), (1, 0)])
    lane = lax.broadcasted_iota(jnp.int32, mine.shape, mine.ndim - 1)
    return jnp.where((lane < G) == (core == 0), mine, jnp.roll(other, G, axis=-1))


def moves():
    return [(z * NY + y, ((z & 1) * NY + y) * NY + (z >> 1)) for z in range(NZ) for y in range(NY)]


def ring(size, step):
    return [(i, (i + step) % size) for i in range(size)]


def sum_over_slab(value):
    value = value + lax.ppermute(value, "core", ring(2, 1))
    near = lax.ppermute(value, "y", ring(NY, 1))
    back = lax.ppermute(value, "y", ring(NY, 3))
    far = lax.ppermute(value, "y", ring(NY, 2))
    return (value + far) + (near + back)


def local(orbitals, pair_table):
    z, x, y, core = (lax.axis_index(a) for a in ("z", "x", "y", "core"))
    mine = orbitals[0]
    live = pair_table[:, 0] >= 0
    code = jnp.where(live, pair_table[:, 0] + 32 * pair_table[:, 1] + 1024 * pair_table[:, 2], -1)
    z_couples = lax.all_gather(orbitals, "z", axis=0, tiled=True)
    own = lane_exchange(mine, core)
    spread = jnp.broadcast_to(own[None], (NX * NY,) + own.shape)
    left = lax.all_to_all(spread, ("x", "y"), split_axis=0, concat_axis=0, tiled=True)
    codes = lax.all_gather(code[None], ("z", "x"), axis=0, tiled=True)

    me = (z * 16 + x * 4 + y).astype(jnp.int32).reshape(1)
    tasks = pl.pallas_call(
        assign_kernel,
        out_shape=jax.ShapeDtypeStruct((17,), jnp.int32),
        in_specs=smem_specs(2),
        out_specs=pl.BlockSpec(memory_space=pltpu.SMEM),
        scratch_shapes=[pltpu.SMEM((NZ * NX * NY,), jnp.int32)],
        cost_estimate=pl.CostEstimate(flops=0, bytes_accessed=60 * 1000 * 1000, transcendentals=0),
        name="assign",
    )(me, codes)
    z_couples, tasks = lax.optimization_barrier((z_couples, tasks))
    phi_all = lax.all_gather(z_couples, "x", axis=0, tiled=True)
    y_couples, left = lax.optimization_barrier((z_couples, left))
    right = lax.all_to_all(y_couples, "y", split_axis=0, concat_axis=0, tiled=True)
    right_other = lax.ppermute(right, "core", ring(2, 1))
    core_id = core.astype(jnp.int32).reshape(1)

    w_depth, w_rows, w_planes = (jnp.asarray(w) for w in weights())
    lacc, sacc, cacc = pl.pallas_call(
        pairs_kernel,
        out_shape=tuple(jax.ShapeDtypeStruct((k, ROWS, 128), f32) for k in (4, 2, 2)),
        in_specs=smem_specs(2) + vmem_specs(7),
        out_specs=tuple(vmem_specs(3)),
        scratch_shapes=[pltpu.VMEM((ROWS, 128), f32)] + [pltpu.VMEM((2, ROWS, 128), bf16)] * 2,
        compiler_params=pltpu.CompilerParams(vmem_limit_bytes=48 * 1024 * 1024),
        cost_estimate=pl.CostEstimate(flops=0, bytes_accessed=60 * 1000 * 1000, transcendentals=0),
        name="pairs",
    )(
        core_id,
        tasks,
        left.reshape(4, ROWS, 128),
        right.reshape(8, 512, 128),
        right_other.reshape(8, 512, 128),
        w_depth,
        w_rows,
        w_planes,
        coulomb(),
    )

    other = lax.ppermute(cacc, "core", ring(2, 1))
    right_parts = quantize_right(z, sacc.reshape(NZ, 512, 128), other.reshape(NZ, 512, 128))
    left_parts = quantize_left(lacc.reshape(NX * NY, 512, 128))
    left_parts, *right_parts = lax.optimization_barrier((left_parts, *right_parts))
    left_parts = lax.all_to_all(left_parts, ("x", "y"), split_axis=0, concat_axis=0, tiled=True)
    right_parts = [
        lax.ppermute(part, "z", ring(NZ, k)) if k else part for k, part in enumerate(right_parts)
    ]
    from_right = lax.ppermute(combine_right(right_parts), ("z", "y"), [(d, s) for s, d in moves()])
    action = combine(left_parts, from_right)
    action_other = lax.ppermute(action, "core", ring(2, 1))

    phi_rows = phi_all.reshape(COUPLES, 512, 128)
    slab_action, over = pl.pallas_call(
        overlap_kernel,
        out_shape=(
            jax.ShapeDtypeStruct((512, 128), f32),
            jax.ShapeDtypeStruct((2 * COUPLES, 128), f32),
        ),
        in_specs=smem_specs(1) + vmem_specs(3),
        out_specs=tuple(vmem_specs(2)),
        scratch_shapes=[pltpu.VMEM((COUPLES, 8, 128), f32)] * 2,
        name="overlap",
    )(core_id, action, action_other, phi_rows)
    out = pl.pallas_call(
        project_kernel,
        out_shape=jax.ShapeDtypeStruct((512, 128), f32),
        in_specs=vmem_specs(3),
        out_specs=vmem_specs(1)[0],
        scratch_shapes=[pltpu.VMEM((2, COUPLES, 128), f32)],
        name="project",
    )(slab_action, phi_rows, sum_over_slab(over))
    return out.reshape(1, 8, G, 128)


def solution(mesh):
    grid = Mesh(mesh.devices.reshape(NZ, NX, NY, 2), ("z", "x", "y", "core"))
    placed = (P(("z", "x"), ("y", "core"), None, None), P(("z", "x"), None))
    return jax.shard_map(
        local,
        mesh=grid,
        in_specs=placed,
        out_specs=P(("z", "x"), ("y", "core"), None, None),
        check_vma=False,
    )
```

```python
import math

import jax
import jax.numpy as jnp
import ml_dtypes
import numpy as np
from jax import lax
from jax.experimental import pallas as pl
from jax.experimental.pallas import tpu as pltpu
from jax.sharding import Mesh
from jax.sharding import PartitionSpec as P

G = 64
ROWS = 2048
CHUNK = 256
KY_STEP = 32
NZ, NX, NY = 8, 4, 4
UNROLL = (8, 2, 8)
COUPLES = 32
CELLS = G * G * G
CODES = 64
FULL = 32500.0
exchange_fraction = 0.25
cell_ratio = 8.0
f32, bf16 = jnp.float32, jnp.bfloat16


def split_np(mat):
    high = mat.astype(ml_dtypes.bfloat16)
    low = (mat - high.astype(np.float64)).astype(ml_dtypes.bfloat16)
    return high, low


def plane_order():
    r = np.arange(32)
    return [16 * (r // 8) + 8 * h + r % 8 for h in (0, 1)]


def weights():
    idx = np.arange(G)
    angles = 2.0 * np.pi / G * (idx[:, None] * idx[None, :] % G)
    hart = (np.cos(angles) + np.sin(angles)) / math.sqrt(G)
    high, low = split_np(np.kron(np.eye(2), hart))
    zero = np.zeros_like(high)
    w_depth = np.block([[high, low], [high, zero]])
    w_rows = np.block([[high, high], [low, zero]])
    order = np.concatenate(plane_order())
    high, low = split_np(hart[np.ix_(order, order)])
    w_planes = np.block([[high, high], [low, np.zeros_like(high)]])
    return w_depth, w_rows, w_planes


def coulomb():
    def folded(v):
        return jnp.minimum(v, G - v).astype(f32)

    pair = lax.broadcasted_iota(jnp.int32, (G // 2, G, 128), 0)
    row = lax.broadcasted_iota(jnp.int32, (G // 2, G, 128), 1)
    lane = lax.broadcasted_iota(jnp.int32, (G // 2, G, 128), 2)
    ky = folded(2 * pair + lane // G)
    kx = cell_ratio * folded(16 * (row % 32 // 8) + 8 * (row // 32) + row % 8)
    kz = folded(lane % G)
    scale = (2.0 * math.pi / G) * (2.0 * math.pi / G)
    squared = scale * (kx * kx + ky * ky + kz * kz)
    safe = jnp.where(squared > 0, squared, 1.0)
    return jnp.where(squared > 0, -exchange_fraction / safe, 0.0)


def packed_slots(left_id, right_id):
    m = left_id.astype(jnp.int32)
    rest = right_id.astype(jnp.int32)
    n, flip = rest & 31, rest >> 5
    mz, mx, nz, nx = m >> 2, m & 3, n >> 2, n & 3
    shared = 8 * flip + 16 * (m == n).astype(jnp.int32)
    first = (mz * 16 + nx * 4 + (nz >> 1)) | (mx + 4 * (nz & 1) + shared) << 7
    second = (nz * 16 + mx * 4 + (mz >> 1)) | (nx + 4 * (mz & 1) + shared) << 7
    return jnp.where(m >= 0, first | second << 16, -1)


def assign_kernel(me_ref, slots_ref, out_ref, load_ref):
    me = me_ref[0]

    def clear(i, carry):
        load_ref[i] = 0
        return carry

    lax.fori_loop(0, NZ * NX * NY, clear, 0, unroll=8)

    def one_block(b, count):
        row = ((me_ref[1] - (b & 3)) & 3) * NZ + (b >> 2)

        def step(state):
            s, slot, cnt = state
            first = slot & 127
            second = (slot >> 16) & 127
            load_a = load_ref[first]
            load_b = load_ref[second]
            use_a = load_a <= load_b
            chip = jnp.where(use_a, first, second)
            load_ref[chip] = jnp.minimum(load_a, load_b) + 1
            out_ref[1 + cnt] = jnp.where(use_a, slot >> 7, slot >> 23) & 31
            slot = jnp.where(s < 31, slots_ref[row, jnp.minimum(s + 1, 31)], -1)
            return s + 1, slot, cnt + (chip == me).astype(jnp.int32)

        return lax.while_loop(lambda state: state[1] >= 0, step, (0, slots_ref[row, 0], count))[2]

    out_ref[0] = lax.fori_loop(0, 32, one_block, 0)


def split(value):
    high = value.astype(bf16)
    return high, (value - high.astype(f32)).astype(bf16)


def depth_transform(value, w_depth):
    high, low = split(value)
    out = jnp.dot(jnp.concatenate([high, low], axis=1), w_depth, preferred_element_type=f32)
    return out[:, :128] + out[:, 128:]


def rows_transform(value, w_rows):
    high, low = split(value)
    half = CHUNK // 2
    top = jnp.concatenate([high[:half], high[half:]], axis=1)
    bottom = jnp.concatenate([low[:half], low[half:]], axis=1)
    out = jnp.dot(w_rows, jnp.concatenate([top, bottom], axis=0), preferred_element_type=f32)
    out = out[:half] + out[half:]
    return jnp.concatenate([out[:, :128], out[:, 128:]], axis=0)


def planes_transform(value, w_planes):
    high, low = split(value)
    out = jnp.dot(w_planes, jnp.concatenate([high, low], axis=0), preferred_element_type=f32)
    return out[:G] + out[G:]


def gather_planes(t_ref, first, low_lanes):
    tops, bottoms = [], []
    for base in range(0, KY_STEP, 8):
        block = jnp.concatenate(
            [t_ref[pl.ds(pl.multiple_of(r * G + first + base, 8), 8)][None] for r in range(32)], axis=0
        )
        block = jnp.swapaxes(block, 0, 1)
        for p in range(0, 8, 2):
            tops.append(jnp.where(low_lanes, block[p], pltpu.roll(block[p + 1], G, 1)))
            bottoms.append(jnp.where(low_lanes, pltpu.roll(block[p], G, 1), block[p + 1]))
    return jnp.concatenate([jnp.concatenate(tops, axis=1), jnp.concatenate(bottoms, axis=1)], axis=0)


def scatter_planes(t_ref, first, value, low_lanes):
    for base in range(0, KY_STEP, 8):
        rows = []
        for p in range(base // 2, base // 2 + 4):
            top = value[:32, p * 128 : (p + 1) * 128]
            bottom = value[32:, p * 128 : (p + 1) * 128]
            rows.append(jnp.where(low_lanes, top, pltpu.roll(bottom, G, 1))[None])
            rows.append(jnp.where(low_lanes, pltpu.roll(top, G, 1), bottom)[None])
        block = jnp.swapaxes(jnp.concatenate(rows, axis=0), 0, 1)
        for r in range(32):
            t_ref[pl.ds(pl.multiple_of(r * G + first + base, 8), 8)] = block[r]


def quantize_piece(value_of, write):
    codes = []
    for p in range(8):
        rows = pl.ds(p * G, G)
        value = value_of(p)
        largest = jnp.max(jnp.abs(value), axis=0, keepdims=True)
        code = jnp.ceil(jnp.log2(jnp.maximum(largest, 1e-30)) * CODES)
        codes.append(code)
        value = jnp.round(value * (jnp.exp2(code * (-1.0 / CODES)) * FULL))
        write(rows, value.astype(jnp.int32).astype(jnp.int16))
    codes = jnp.concatenate(codes + [jnp.zeros((8, 128), f32)], axis=0)
    write(pl.ds(512, 16), codes.astype(jnp.int32).astype(jnp.int16))


def pairs_kernel(
    ids_ref,
    tasks_ref,
    left_ref,
    mine0_ref,
    mine1_ref,
    mine2_ref,
    mine3_ref,
    other0_ref,
    other1_ref,
    other2_ref,
    other3_ref,
    wz_ref,
    wy_ref,
    wx_ref,
    kern_ref,
    left_out_ref,
    sacc_ref,
    cacc_ref,
    t_ref,
    same_ref,
    cross_ref,
    lacc_ref,
):
    def clear(i, carry):
        rows = pl.ds(pl.multiple_of(i * CHUNK, CHUNK), CHUNK)
        for k in range(4):
            lacc_ref[k, rows] = jnp.zeros((CHUNK, 128), f32)
        for k in range(2):
            sacc_ref[k, rows] = jnp.zeros((CHUNK, 128), f32)
            cacc_ref[k, rows] = jnp.zeros((CHUNK, 128), f32)
        return carry

    lax.fori_loop(0, ROWS // CHUNK, clear, 0)
    keep = (lax.broadcasted_iota(jnp.int32, (G, 128), 1) < G) == (ids_ref[0] == 0)
    mine_refs = (mine0_ref, mine1_ref, mine2_ref, mine3_ref)
    other_refs = (other0_ref, other1_ref, other2_ref, other3_ref)

    def exchange(i, carry):
        source = pl.ds(pl.multiple_of(i * G, G), G)
        for k in range(NY):
            quarter = (ids_ref[1] - k) & (NY - 1)
            rows = pl.ds(pl.multiple_of(quarter * 512 + i * G, G), G)
            for j in range(2):
                mine = mine_refs[k][j, source].astype(f32)
                other = other_refs[k][j, source].astype(f32)
                same_ref[j, rows] = jnp.where(keep, mine, pltpu.roll(other, G, 1)).astype(bf16)
                cross_ref[j, rows] = jnp.where(keep, pltpu.roll(mine, G, 1), other).astype(bf16)
        return carry

    lax.fori_loop(0, 8, exchange, 0)
    low_lanes = lax.broadcasted_iota(jnp.int32, (32, 128), 1) < G

    def run(right_ref, racc_ref, task):
        a = task & 3
        b = (task >> 2) & 1
        second = 1.0 - (task >> 4).astype(f32)

        def forward(i, c):
            rows = pl.ds(pl.multiple_of(i * CHUNK, CHUNK), CHUNK)
            rho = left_ref[a, rows].astype(f32) * right_ref[b, rows].astype(f32)
            t_ref[rows] = rows_transform(depth_transform(rho, wz_ref[...]), wy_ref[...])
            return c

        lax.fori_loop(0, ROWS // CHUNK, forward, 0, unroll=UNROLL[0])

        def middle(i, c):
            first = pl.multiple_of(i * KY_STEP, KY_STEP)
            value = gather_planes(t_ref, first, low_lanes)
            kern = jnp.concatenate(
                [kern_ref[i * (KY_STEP // 2) + j] for j in range(KY_STEP // 2)], axis=1
            )
            value = planes_transform(value, wx_ref[...]) * kern
            value = planes_transform(value, wx_ref[...])
            scatter_planes(t_ref, first, value, low_lanes)
            return c

        lax.fori_loop(0, G // KY_STEP, middle, 0, unroll=UNROLL[1])

        def backward(i, c):
            rows = pl.ds(pl.multiple_of(i * CHUNK, CHUNK), CHUNK)
            v = depth_transform(rows_transform(t_ref[rows], wy_ref[...]), wz_ref[...])
            lacc_ref[a, rows] += v * right_ref[b, rows].astype(f32)
            racc_ref[b, rows] += (v * second) * left_ref[a, rows].astype(f32)
            return c

        lax.fori_loop(0, ROWS // CHUNK, backward, 0, unroll=UNROLL[2])

    def one_task(t, carry):
        task = tasks_ref[1 + t]
        flipped = (task >> 3) & 1 == 1

        @pl.when(jnp.logical_not(flipped))
        def _():
            run(same_ref, sacc_ref, task)

        @pl.when(flipped)
        def _():
            run(cross_ref, cacc_ref, task)

        return carry

    lax.fori_loop(0, tasks_ref[0], one_task, 0)

    def quantize_left(k, carry):
        def write(rows, value):
            left_out_ref[k, rows] = value

        def value_of(p):
            return lacc_ref[k // NY, pl.ds(pl.multiple_of((k % NY) * 512 + p * G, G), G)]

        quantize_piece(value_of, write)
        return carry

    lax.fori_loop(0, NX * NY, quantize_left, 0)


def quantize_right_kernel(z_ref, first_ref, second_ref, *out_refs):
    for k in range(NZ):
        piece = (z_ref[0] + k) & (NZ - 1)

        def write(rows, value):
            out_refs[k][rows] = value

        def value_of(p):
            rows = pl.ds(p * G, G)
            return first_ref[piece, rows] + second_ref[piece, rows]

        quantize_piece(value_of, write)


def piece_sum(parts):
    def read(part, rows):
        return part[rows].astype(jnp.int32).astype(f32)

    scales = [jnp.exp2(read(part, pl.ds(512, 16))[:8] * (1.0 / CODES)) * (1.0 / FULL) for part in parts]

    def value_of(p):
        total = jnp.zeros((G, 128), f32)
        for part, scale in zip(parts, scales):
            total = total + read(part, pl.ds(p * G, G)) * scale[p : p + 1]
        return total

    return value_of


def combine_kernel(left_ref, right_ref, out_ref):
    value_of = piece_sum([left_ref.at[k] for k in range(NX * NY)] + [right_ref])
    for p in range(8):
        out_ref[pl.ds(p * G, G)] = value_of(p)


def combine_right_kernel(*refs):
    value_of = piece_sum(refs[:-1])

    def write(rows, value):
        refs[-1][rows] = value

    quantize_piece(value_of, write)


def quantize_right(z, first, second):
    return pl.pallas_call(
        quantize_right_kernel,
        out_shape=(jax.ShapeDtypeStruct((528, 128), jnp.int16),) * NZ,
        in_specs=smem_specs(1) + vmem_specs(2),
        out_specs=tuple(vmem_specs(NZ)),
        cost_estimate=pl.CostEstimate(flops=0, bytes_accessed=8 * 1000 * 1000, transcendentals=0),
        name="quantize_right",
    )(z.astype(jnp.int32).reshape(1), first, second)


def combine(left_parts, right_part):
    return pl.pallas_call(
        combine_kernel,
        out_shape=jax.ShapeDtypeStruct((512, 128), f32),
        in_specs=vmem_specs(2),
        out_specs=vmem_specs(1)[0],
        name="combine",
    )(left_parts, right_part)


def combine_right(parts):
    return pl.pallas_call(
        combine_right_kernel,
        out_shape=jax.ShapeDtypeStruct((528, 128), jnp.int16),
        in_specs=vmem_specs(len(parts)),
        out_specs=vmem_specs(1)[0],
        cost_estimate=pl.CostEstimate(flops=0, bytes_accessed=6 * 1000 * 1000, transcendentals=0),
        name="combine_right",
    )(*parts)


def overlap_kernel(core_ref, own_ref, other_ref, phi_ref, x_ref, out_ref, same_ref, cross_ref):
    keep = (lax.broadcasted_iota(jnp.int32, (G, 128), 1) < G) == (core_ref[0] == 0)
    same_ref[...] = jnp.zeros_like(same_ref)
    cross_ref[...] = jnp.zeros_like(cross_ref)

    def rows_block(i, carry):
        rows = pl.ds(pl.multiple_of(i * G, G), G)
        value = jnp.where(keep, own_ref[rows], pltpu.roll(other_ref[rows], G, 1))
        turned = pltpu.roll(value, G, 1)
        x_ref[rows] = value
        for o in range(COUPLES):
            phi = phi_ref[o, rows].astype(f32)
            same_ref[o] += jnp.sum((phi * value).reshape(8, 8, 128), axis=0)
            cross_ref[o] += jnp.sum((phi * turned).reshape(8, 8, 128), axis=0)
        return carry

    lax.fori_loop(0, 8, rows_block, 0)
    out_ref[pl.ds(0, COUPLES)] = jnp.sum(same_ref[...], axis=1)
    out_ref[pl.ds(COUPLES, COUPLES)] = jnp.sum(cross_ref[...], axis=1)


def project_kernel(x_ref, phi_ref, over0_ref, over1_ref, over2_ref, over3_ref, out_ref, coef_ref):
    lane = lax.broadcasted_iota(jnp.int32, (COUPLES, 128), 1)
    for k in range(2):
        half = pl.ds(k * COUPLES, COUPLES)
        part = (over0_ref[half] + over2_ref[half]) + (over1_ref[half] + over3_ref[half])
        low = jnp.sum(jnp.where(lane < G, part, 0.0), axis=1, keepdims=True)
        high = jnp.sum(jnp.where(lane < G, 0.0, part), axis=1, keepdims=True)
        coef_ref[k] = jnp.where(lane < G, low, high) / CELLS

    def rows_block(i, carry):
        rows = pl.ds(pl.multiple_of(i * G, G), G)
        same = jnp.zeros((G, 128), f32)
        cross = jnp.zeros((G, 128), f32)
        for o in range(COUPLES):
            phi = phi_ref[o, rows].astype(f32)
            same = same + phi * coef_ref[0, o : o + 1]
            cross = cross + phi * coef_ref[1, o : o + 1]
        out_ref[rows] = x_ref[rows] - same - pltpu.roll(cross, G, 1)
        return carry

    lax.fori_loop(0, 8, rows_block, 0)


def vmem_specs(n):
    return [pl.BlockSpec(memory_space=pltpu.VMEM)] * n


def smem_specs(n):
    return [pl.BlockSpec(memory_space=pltpu.SMEM)] * n


def lane_exchange(mine, core):
    other = lax.ppermute(mine, "core", [(0, 1), (1, 0)])
    lane = lax.broadcasted_iota(jnp.int32, mine.shape, mine.ndim - 1)
    return jnp.where((lane < G) == (core == 0), mine, jnp.roll(other, G, axis=-1))


def moves():
    return [(z * NY + y, ((z & 1) * NY + y) * NY + (z >> 1)) for z in range(NZ) for y in range(NY)]


def ring(size, step):
    return [(i, (i + step) % size) for i in range(size)]


def over_y(value):
    return [value] + [lax.ppermute(value, "y", ring(NY, k)) for k in range(1, NY)]


def local(orbitals, pair_table):
    z, x, y, core = (lax.axis_index(a) for a in ("z", "x", "y", "core"))
    mine = orbitals[0]
    slots = jnp.concatenate([pair_table[:, 0], pair_table[:, 1] + 32 * pair_table[:, 2]])
    slots = jnp.pad(slots.astype(bf16)[None], ((0, 15), (0, 64)))
    z_couples = jnp.concatenate([mine.reshape(512, 128), slots], axis=0)[None]
    z_couples = lax.all_gather(z_couples, "z", axis=0, tiled=True)
    own = lane_exchange(mine, core)
    spread = jnp.broadcast_to(own[None], (NX * NY,) + own.shape)
    left = lax.all_to_all(spread, ("x", "y"), split_axis=0, concat_axis=0, tiled=True)

    z_couples, left = lax.optimization_barrier((z_couples, left))
    slots = z_couples[:, 512, :]
    slots = jnp.concatenate([slots] + [lax.ppermute(slots, "x", ring(NX, k)) for k in range(1, NX)])
    slots = packed_slots(slots[:, :32], slots[:, 32:64])
    me = jnp.stack([z * 16 + x * 4 + y, x]).astype(jnp.int32)
    tasks = pl.pallas_call(
        assign_kernel,
        out_shape=jax.ShapeDtypeStruct((18,), jnp.int32),
        in_specs=smem_specs(2),
        out_specs=pl.BlockSpec(memory_space=pltpu.SMEM),
        scratch_shapes=[pltpu.SMEM((NZ * NX * NY,), jnp.int32)],
        cost_estimate=pl.CostEstimate(flops=0, bytes_accessed=60 * 1000 * 1000, transcendentals=0),
        name="assign",
    )(me, slots)
    phi_all = lax.all_gather(z_couples, "x", axis=0, tiled=True)
    right = []
    for k in range(NY):
        part = lax.dynamic_slice(z_couples, (2 * ((y + k) % NY), 0, 0), (2, 512, 128))
        right.append(lax.ppermute(part, "y", ring(NY, k)) if k else part)
    right_other = [lax.ppermute(part, "core", ring(2, 1)) for part in right]
    ids = jnp.stack([core, y]).astype(jnp.int32)

    w_depth, w_rows, w_planes = (jnp.asarray(w) for w in weights())
    left_parts, sacc, cacc = pl.pallas_call(
        pairs_kernel,
        out_shape=(
            jax.ShapeDtypeStruct((NX * NY, 528, 128), jnp.int16),
            jax.ShapeDtypeStruct((2, ROWS, 128), f32),
            jax.ShapeDtypeStruct((2, ROWS, 128), f32),
        ),
        in_specs=smem_specs(2) + vmem_specs(5 + 2 * NY),
        out_specs=tuple(vmem_specs(3)),
        scratch_shapes=[
            pltpu.VMEM((ROWS, 128), f32),
            pltpu.VMEM((2, ROWS, 128), bf16),
            pltpu.VMEM((2, ROWS, 128), bf16),
            pltpu.VMEM((4, ROWS, 128), f32),
        ],
        compiler_params=pltpu.CompilerParams(vmem_limit_bytes=48 * 1024 * 1024),
        cost_estimate=pl.CostEstimate(flops=0, bytes_accessed=60 * 1000 * 1000, transcendentals=0),
        name="pairs",
    )(
        ids,
        tasks,
        left.reshape(4, ROWS, 128),
        *right,
        *right_other,
        w_depth,
        w_rows,
        w_planes,
        coulomb(),
    )

    other = lax.ppermute(cacc, "core", ring(2, 1))
    right_parts = quantize_right(z, sacc.reshape(NZ, 512, 128), other.reshape(NZ, 512, 128))
    left_parts = lax.all_to_all(left_parts, ("x", "y"), split_axis=0, concat_axis=0, tiled=True)
    right_parts = [
        lax.ppermute(part, "z", ring(NZ, k)) if k else part for k, part in enumerate(right_parts)
    ]
    from_right = lax.ppermute(combine_right(right_parts), ("z", "y"), [(d, s) for s, d in moves()])
    action = combine(left_parts, from_right)
    action_other = lax.ppermute(action, "core", ring(2, 1))

    slab_action, over = pl.pallas_call(
        overlap_kernel,
        out_shape=(
            jax.ShapeDtypeStruct((512, 128), f32),
            jax.ShapeDtypeStruct((2 * COUPLES, 128), f32),
        ),
        in_specs=smem_specs(1) + vmem_specs(3),
        out_specs=tuple(vmem_specs(2)),
        scratch_shapes=[pltpu.VMEM((COUPLES, 8, 128), f32)] * 2,
        name="overlap",
    )(ids, action, action_other, phi_all)
    out = pl.pallas_call(
        project_kernel,
        out_shape=jax.ShapeDtypeStruct((512, 128), f32),
        in_specs=vmem_specs(2 + NY),
        out_specs=vmem_specs(1)[0],
        scratch_shapes=[pltpu.VMEM((2, COUPLES, 128), f32)],
        name="project",
    )(slab_action, phi_all, *over_y(over + lax.ppermute(over, "core", ring(2, 1))))
    return out.reshape(1, 8, G, 128)


def solution(mesh):
    grid = Mesh(mesh.devices.reshape(NZ, NX, NY, 2), ("z", "x", "y", "core"))
    placed = (P(("z", "x"), ("y", "core"), None, None), P(("z", "x"), None))
    return jax.shard_map(
        local,
        mesh=grid,
        in_specs=placed,
        out_specs=P(("z", "x"), ("y", "core"), None, None),
        check_vma=False,
    )
```

```python
import math

import jax
import jax.numpy as jnp
import ml_dtypes
import numpy as np
from jax import lax
from jax.experimental import pallas as pl
from jax.experimental.pallas import tpu as pltpu
from jax.sharding import Mesh
from jax.sharding import PartitionSpec as P

G = 64
ROWS = 2048
CHUNK = 256
KY_STEP = 32
NZ, NX, NY = 8, 4, 4
UNROLL = (8, 2, 8)
COUPLES = 32
CELLS = G * G * G
CODES = 64
FULL = 32500.0
exchange_fraction = 0.25
cell_ratio = 8.0
f32, bf16 = jnp.float32, jnp.bfloat16


def split_np(mat):
    high = mat.astype(ml_dtypes.bfloat16)
    low = (mat - high.astype(np.float64)).astype(ml_dtypes.bfloat16)
    return high, low


def plane_order():
    r = np.arange(32)
    return [16 * (r // 8) + 8 * h + r % 8 for h in (0, 1)]


def weights():
    idx = np.arange(G)
    angles = 2.0 * np.pi / G * (idx[:, None] * idx[None, :] % G)
    hart = (np.cos(angles) + np.sin(angles)) / math.sqrt(G)
    high, low = split_np(np.kron(np.eye(2), hart))
    zero = np.zeros_like(high)
    w_depth = np.block([[high, low], [high, zero]])
    w_rows = np.block([[high, high], [low, zero]])
    order = np.concatenate(plane_order())
    high, low = split_np(hart[np.ix_(order, order)])
    w_planes = np.block([[high, high], [low, np.zeros_like(high)]])
    return w_depth, w_rows, w_planes


def coulomb():
    def folded(v):
        return jnp.minimum(v, G - v).astype(f32)

    pair = lax.broadcasted_iota(jnp.int32, (G // 2, G, 128), 0)
    row = lax.broadcasted_iota(jnp.int32, (G // 2, G, 128), 1)
    lane = lax.broadcasted_iota(jnp.int32, (G // 2, G, 128), 2)
    ky = folded(2 * pair + lane // G)
    kx = cell_ratio * folded(16 * (row % 32 // 8) + 8 * (row // 32) + row % 8)
    kz = folded(lane % G)
    scale = (2.0 * math.pi / G) * (2.0 * math.pi / G)
    squared = scale * (kx * kx + ky * ky + kz * kz)
    safe = jnp.where(squared > 0, squared, 1.0)
    return jnp.where(squared > 0, -exchange_fraction / safe, 0.0)


def packed_slots(left_id, right_id):
    m = left_id.astype(jnp.int32)
    rest = right_id.astype(jnp.int32)
    n, flip = rest & 31, rest >> 5
    mz, mx, nz, nx = m >> 2, m & 3, n >> 2, n & 3
    shared = 8 * flip + 16 * (m == n).astype(jnp.int32)
    first = (mz * 16 + nx * 4 + (nz >> 1)) | (mx + 4 * (nz & 1) + shared) << 7
    second = (nz * 16 + mx * 4 + (mz >> 1)) | (nx + 4 * (mz & 1) + shared) << 7
    return jnp.where(m >= 0, first | second << 16, -1)


def assign_kernel(me_ref, slots_ref, out_ref, load_ref):
    me = me_ref[0]

    def clear(i, carry):
        load_ref[i] = 0
        return carry

    lax.fori_loop(0, NZ * NX * NY, clear, 0, unroll=8)

    def one_block(b, count):
        row = ((me_ref[1] - (b & 3)) & 3) * NZ + (b >> 2)

        def step(state):
            s, slot, cnt = state
            first = slot & 127
            second = (slot >> 16) & 127
            load_a = load_ref[first]
            load_b = load_ref[second]
            use_a = load_a <= load_b
            chip = jnp.where(use_a, first, second)
            load_ref[chip] = jnp.minimum(load_a, load_b) + 1
            out_ref[1 + cnt] = jnp.where(use_a, slot >> 7, slot >> 23) & 31
            slot = jnp.where(s < 31, slots_ref[row, jnp.minimum(s + 1, 31)], -1)
            return s + 1, slot, cnt + (chip == me).astype(jnp.int32)

        return lax.while_loop(lambda state: state[1] >= 0, step, (0, slots_ref[row, 0], count))[2]

    out_ref[0] = lax.fori_loop(0, 32, one_block, 0)


def split(value):
    high = value.astype(bf16)
    return high, (value - high.astype(f32)).astype(bf16)


def depth_transform(value, w_depth):
    high, low = split(value)
    out = jnp.dot(jnp.concatenate([high, low], axis=1), w_depth, preferred_element_type=f32)
    return out[:, :128] + out[:, 128:]


def rows_transform(value, w_rows):
    high, low = split(value)
    half = CHUNK // 2
    top = jnp.concatenate([high[:half], high[half:]], axis=1)
    bottom = jnp.concatenate([low[:half], low[half:]], axis=1)
    out = jnp.dot(w_rows, jnp.concatenate([top, bottom], axis=0), preferred_element_type=f32)
    out = out[:half] + out[half:]
    return jnp.concatenate([out[:, :128], out[:, 128:]], axis=0)


def planes_transform(value, w_planes):
    high, low = split(value)
    out = jnp.dot(w_planes, jnp.concatenate([high, low], axis=0), preferred_element_type=f32)
    return out[:G] + out[G:]


def gather_planes(t_ref, first, low_lanes):
    tops, bottoms = [], []
    for base in range(0, KY_STEP, 8):
        block = jnp.concatenate(
            [t_ref[pl.ds(pl.multiple_of(r * G + first + base, 8), 8)][None] for r in range(32)], axis=0
        )
        block = jnp.swapaxes(block, 0, 1)
        for p in range(0, 8, 2):
            tops.append(jnp.where(low_lanes, block[p], pltpu.roll(block[p + 1], G, 1)))
            bottoms.append(jnp.where(low_lanes, pltpu.roll(block[p], G, 1), block[p + 1]))
    return jnp.concatenate([jnp.concatenate(tops, axis=1), jnp.concatenate(bottoms, axis=1)], axis=0)


def scatter_planes(t_ref, first, value, low_lanes):
    for base in range(0, KY_STEP, 8):
        rows = []
        for p in range(base // 2, base // 2 + 4):
            top = value[:32, p * 128 : (p + 1) * 128]
            bottom = value[32:, p * 128 : (p + 1) * 128]
            rows.append(jnp.where(low_lanes, top, pltpu.roll(bottom, G, 1))[None])
            rows.append(jnp.where(low_lanes, pltpu.roll(top, G, 1), bottom)[None])
        block = jnp.swapaxes(jnp.concatenate(rows, axis=0), 0, 1)
        for r in range(32):
            t_ref[pl.ds(pl.multiple_of(r * G + first + base, 8), 8)] = block[r]


def quantize_piece(value_of, write):
    codes = []
    for p in range(8):
        rows = pl.ds(p * G, G)
        value = value_of(p)
        largest = jnp.max(jnp.abs(value), axis=0, keepdims=True)
        code = jnp.ceil(jnp.log2(jnp.maximum(largest, 1e-30)) * CODES)
        codes.append(code)
        value = jnp.round(value * (jnp.exp2(code * (-1.0 / CODES)) * FULL))
        write(rows, value.astype(jnp.int32).astype(jnp.int16))
    codes = jnp.concatenate(codes + [jnp.zeros((8, 128), f32)], axis=0)
    write(pl.ds(512, 16), codes.astype(jnp.int32).astype(jnp.int16))


def pairs_kernel(
    ids_ref,
    tasks_ref,
    left_ref,
    mine0_ref,
    mine1_ref,
    mine2_ref,
    mine3_ref,
    other0_ref,
    other1_ref,
    other2_ref,
    other3_ref,
    wz_ref,
    wy_ref,
    wx_ref,
    kern_ref,
    left_out_ref,
    sacc_ref,
    cacc_ref,
    t_ref,
    same_ref,
    cross_ref,
    lacc_ref,
):
    def clear(i, carry):
        rows = pl.ds(pl.multiple_of(i * CHUNK, CHUNK), CHUNK)
        for k in range(4):
            lacc_ref[k, rows] = jnp.zeros((CHUNK, 128), f32)
        for k in range(2):
            sacc_ref[k, rows] = jnp.zeros((CHUNK, 128), f32)
            cacc_ref[k, rows] = jnp.zeros((CHUNK, 128), f32)
        return carry

    lax.fori_loop(0, ROWS // CHUNK, clear, 0)
    keep = (lax.broadcasted_iota(jnp.int32, (G, 128), 1) < G) == (ids_ref[0] == 0)
    mine_refs = (mine0_ref, mine1_ref, mine2_ref, mine3_ref)
    other_refs = (other0_ref, other1_ref, other2_ref, other3_ref)

    def exchange(i, carry):
        source = pl.ds(pl.multiple_of(i * G, G), G)
        for k in range(NY):
            quarter = (ids_ref[1] - k) & (NY - 1)
            rows = pl.ds(pl.multiple_of(quarter * 512 + i * G, G), G)
            for j in range(2):
                mine = mine_refs[k][j, source].astype(f32)
                other = other_refs[k][j, source].astype(f32)
                same_ref[j, rows] = jnp.where(keep, mine, pltpu.roll(other, G, 1)).astype(bf16)
                cross_ref[j, rows] = jnp.where(keep, pltpu.roll(mine, G, 1), other).astype(bf16)
        return carry

    lax.fori_loop(0, 8, exchange, 0)
    low_lanes = lax.broadcasted_iota(jnp.int32, (32, 128), 1) < G

    def run(right_ref, racc_ref, task):
        a = task & 3
        b = (task >> 2) & 1
        second = 1.0 - (task >> 4).astype(f32)

        def forward(i, c):
            rows = pl.ds(pl.multiple_of(i * CHUNK, CHUNK), CHUNK)
            rho = left_ref[a, rows].astype(f32) * right_ref[b, rows].astype(f32)
            t_ref[rows] = rows_transform(depth_transform(rho, wz_ref[...]), wy_ref[...])
            return c

        lax.fori_loop(0, ROWS // CHUNK, forward, 0, unroll=UNROLL[0])

        def middle(i, c):
            first = pl.multiple_of(i * KY_STEP, KY_STEP)
            value = gather_planes(t_ref, first, low_lanes)
            kern = jnp.concatenate(
                [kern_ref[i * (KY_STEP // 2) + j] for j in range(KY_STEP // 2)], axis=1
            )
            value = planes_transform(value, wx_ref[...]) * kern
            value = planes_transform(value, wx_ref[...])
            scatter_planes(t_ref, first, value, low_lanes)
            return c

        lax.fori_loop(0, G // KY_STEP, middle, 0, unroll=UNROLL[1])

        def backward(i, c):
            rows = pl.ds(pl.multiple_of(i * CHUNK, CHUNK), CHUNK)
            v = depth_transform(rows_transform(t_ref[rows], wy_ref[...]), wz_ref[...])
            lacc_ref[a, rows] += v * right_ref[b, rows].astype(f32)
            racc_ref[b, rows] += (v * second) * left_ref[a, rows].astype(f32)
            return c

        lax.fori_loop(0, ROWS // CHUNK, backward, 0, unroll=UNROLL[2])

    def one_task(t, carry):
        task = tasks_ref[1 + t]
        flipped = (task >> 3) & 1 == 1

        @pl.when(jnp.logical_not(flipped))
        def _():
            run(same_ref, sacc_ref, task)

        @pl.when(flipped)
        def _():
            run(cross_ref, cacc_ref, task)

        return carry

    lax.fori_loop(0, tasks_ref[0], one_task, 0)

    def quantize_left(k, carry):
        def write(rows, value):
            left_out_ref[k, rows] = value

        def value_of(p):
            return lacc_ref[k // NY, pl.ds(pl.multiple_of((k % NY) * 512 + p * G, G), G)]

        quantize_piece(value_of, write)
        return carry

    lax.fori_loop(0, NX * NY, quantize_left, 0)


def quantize_right_kernel(zy_ref, first_ref, second_ref, *out_refs):
    for k in range(NZ):
        step = (zy_ref[0] + k - 2 * zy_ref[1]) & (NZ - 1)
        piece = jnp.where((step >= 1) & (step <= NY), step + NY - 1, (NZ - step) & (NZ - 1))

        def write(rows, value):
            out_refs[k][rows] = value

        def value_of(p):
            rows = pl.ds(p * G, G)
            return first_ref[piece, rows] + second_ref[piece, rows]

        quantize_piece(value_of, write)


def piece_sum(parts):
    def read(part, rows):
        return part[rows].astype(jnp.int32).astype(f32)

    scales = [jnp.exp2(read(part, pl.ds(512, 16))[:8] * (1.0 / CODES)) * (1.0 / FULL) for part in parts]

    def value_of(p):
        total = jnp.zeros((G, 128), f32)
        for part, scale in zip(parts, scales):
            total = total + read(part, pl.ds(p * G, G)) * scale[p : p + 1]
        return total

    return value_of


def combine_kernel(left_ref, right_ref, out_ref):
    value_of = piece_sum([left_ref.at[k] for k in range(NX * NY)] + [right_ref])
    for p in range(8):
        out_ref[pl.ds(p * G, G)] = value_of(p)


def combine_right_kernel(*refs):
    value_of = piece_sum(refs[:-1])

    def write(rows, value):
        refs[-1][rows] = value

    quantize_piece(value_of, write)


def quantize_right(zy, first, second):
    return pl.pallas_call(
        quantize_right_kernel,
        out_shape=(jax.ShapeDtypeStruct((528, 128), jnp.int16),) * NZ,
        in_specs=smem_specs(1) + vmem_specs(2),
        out_specs=tuple(vmem_specs(NZ)),
        cost_estimate=pl.CostEstimate(flops=0, bytes_accessed=8 * 1000 * 1000, transcendentals=0),
        name="quantize_right",
    )(zy, first, second)


def combine(left_parts, right_part):
    return pl.pallas_call(
        combine_kernel,
        out_shape=jax.ShapeDtypeStruct((512, 128), f32),
        in_specs=vmem_specs(2),
        out_specs=vmem_specs(1)[0],
        name="combine",
    )(left_parts, right_part)


def combine_right(parts):
    return pl.pallas_call(
        combine_right_kernel,
        out_shape=jax.ShapeDtypeStruct((528, 128), jnp.int16),
        in_specs=vmem_specs(len(parts)),
        out_specs=vmem_specs(1)[0],
        cost_estimate=pl.CostEstimate(flops=0, bytes_accessed=6 * 1000 * 1000, transcendentals=0),
        name="combine_right",
    )(*parts)


def overlap_kernel(core_ref, own_ref, other_ref, phi_ref, x_ref, out_ref, same_ref, cross_ref):
    keep = (lax.broadcasted_iota(jnp.int32, (G, 128), 1) < G) == (core_ref[0] == 0)
    same_ref[...] = jnp.zeros_like(same_ref)
    cross_ref[...] = jnp.zeros_like(cross_ref)

    def rows_block(i, carry):
        rows = pl.ds(pl.multiple_of(i * G, G), G)
        value = jnp.where(keep, own_ref[rows], pltpu.roll(other_ref[rows], G, 1))
        turned = pltpu.roll(value, G, 1)
        x_ref[rows] = value
        for o in range(COUPLES):
            phi = phi_ref[o, rows].astype(f32)
            same_ref[o] += jnp.sum((phi * value).reshape(8, 8, 128), axis=0)
            cross_ref[o] += jnp.sum((phi * turned).reshape(8, 8, 128), axis=0)
        return carry

    lax.fori_loop(0, 8, rows_block, 0)
    out_ref[pl.ds(0, COUPLES)] = jnp.sum(same_ref[...], axis=1)
    out_ref[pl.ds(COUPLES, COUPLES)] = jnp.sum(cross_ref[...], axis=1)


def project_kernel(x_ref, phi_ref, over0_ref, over1_ref, over2_ref, over3_ref, out_ref, coef_ref):
    lane = lax.broadcasted_iota(jnp.int32, (COUPLES, 128), 1)
    for k in range(2):
        half = pl.ds(k * COUPLES, COUPLES)
        part = (over0_ref[half] + over2_ref[half]) + (over1_ref[half] + over3_ref[half])
        low = jnp.sum(jnp.where(lane < G, part, 0.0), axis=1, keepdims=True)
        high = jnp.sum(jnp.where(lane < G, 0.0, part), axis=1, keepdims=True)
        coef_ref[k] = jnp.where(lane < G, low, high) / CELLS

    def rows_block(i, carry):
        rows = pl.ds(pl.multiple_of(i * G, G), G)
        same = jnp.zeros((G, 128), f32)
        cross = jnp.zeros((G, 128), f32)
        for o in range(COUPLES):
            phi = phi_ref[o, rows].astype(f32)
            same = same + phi * coef_ref[0, o : o + 1]
            cross = cross + phi * coef_ref[1, o : o + 1]
        out_ref[rows] = x_ref[rows] - same - pltpu.roll(cross, G, 1)
        return carry

    lax.fori_loop(0, 8, rows_block, 0)


def vmem_specs(n):
    return [pl.BlockSpec(memory_space=pltpu.VMEM)] * n


def smem_specs(n):
    return [pl.BlockSpec(memory_space=pltpu.SMEM)] * n


def lane_exchange(mine, core):
    other = lax.ppermute(mine, "core", [(0, 1), (1, 0)])
    lane = lax.broadcasted_iota(jnp.int32, mine.shape, mine.ndim - 1)
    return jnp.where((lane < G) == (core == 0), mine, jnp.roll(other, G, axis=-1))


def home():
    pairs = []
    for z in range(NZ):
        for q in range(NY):
            y, b = z // 2, z % 2
            holder = (2 * y + (q + 1 if b else -q)) % NZ
            pairs.append((holder * NY + y, z * NY + q))
    return pairs


def ring(size, step):
    return [(i, (i + step) % size) for i in range(size)]


def over_y(value):
    return [value] + [lax.ppermute(value, "y", ring(NY, k)) for k in range(1, NY)]


def local(orbitals, pair_table):
    z, x, y, core = (lax.axis_index(a) for a in ("z", "x", "y", "core"))
    mine = orbitals[0]
    slots = jnp.concatenate([pair_table[:, 0], pair_table[:, 1] + 32 * pair_table[:, 2]])
    slots = jnp.pad(slots.astype(bf16)[None], ((0, 15), (0, 64)))
    z_couples = jnp.concatenate([mine.reshape(512, 128), slots], axis=0)[None]
    z_couples = lax.all_gather(z_couples, "z", axis=0, tiled=True)
    own = lane_exchange(mine, core)
    spread = jnp.broadcast_to(own[None], (NX * NY,) + own.shape)
    left = lax.all_to_all(spread, ("x", "y"), split_axis=0, concat_axis=0, tiled=True)

    z_couples, left = lax.optimization_barrier((z_couples, left))
    slots = z_couples[:, 512, :]
    slots = jnp.concatenate([slots] + [lax.ppermute(slots, "x", ring(NX, k)) for k in range(1, NX)])
    slots = packed_slots(slots[:, :32], slots[:, 32:64])
    me = jnp.stack([z * 16 + x * 4 + y, x]).astype(jnp.int32)
    tasks = pl.pallas_call(
        assign_kernel,
        out_shape=jax.ShapeDtypeStruct((18,), jnp.int32),
        in_specs=smem_specs(2),
        out_specs=pl.BlockSpec(memory_space=pltpu.SMEM),
        scratch_shapes=[pltpu.SMEM((NZ * NX * NY,), jnp.int32)],
        cost_estimate=pl.CostEstimate(flops=0, bytes_accessed=60 * 1000 * 1000, transcendentals=0),
        name="assign",
    )(me, slots)
    phi_all = lax.all_gather(z_couples, "x", axis=0, tiled=True)
    right = []
    for k in range(NY):
        part = lax.dynamic_slice(z_couples, (2 * ((y + k) % NY), 0, 0), (2, 512, 128))
        right.append(lax.ppermute(part, "y", ring(NY, k)) if k else part)
    *right, tasks = lax.optimization_barrier((*right, tasks))
    right_other = [lax.ppermute(part, "core", ring(2, 1)) for part in right]
    ids = jnp.stack([core, y]).astype(jnp.int32)

    w_depth, w_rows, w_planes = (jnp.asarray(w) for w in weights())
    left_parts, sacc, cacc = pl.pallas_call(
        pairs_kernel,
        out_shape=(
            jax.ShapeDtypeStruct((NX * NY, 528, 128), jnp.int16),
            jax.ShapeDtypeStruct((2, ROWS, 128), f32),
            jax.ShapeDtypeStruct((2, ROWS, 128), f32),
        ),
        in_specs=smem_specs(2) + vmem_specs(5 + 2 * NY),
        out_specs=tuple(vmem_specs(3)),
        scratch_shapes=[
            pltpu.VMEM((ROWS, 128), f32),
            pltpu.VMEM((2, ROWS, 128), bf16),
            pltpu.VMEM((2, ROWS, 128), bf16),
            pltpu.VMEM((4, ROWS, 128), f32),
        ],
        compiler_params=pltpu.CompilerParams(vmem_limit_bytes=48 * 1024 * 1024),
        cost_estimate=pl.CostEstimate(flops=0, bytes_accessed=60 * 1000 * 1000, transcendentals=0),
        name="pairs",
    )(
        ids,
        tasks,
        left.reshape(4, ROWS, 128),
        *right,
        *right_other,
        w_depth,
        w_rows,
        w_planes,
        coulomb(),
    )

    other = lax.ppermute(cacc, "core", ring(2, 1))
    right_parts = quantize_right(jnp.stack([z, y]).astype(jnp.int32), sacc.reshape(NZ, 512, 128), other.reshape(NZ, 512, 128))
    left_parts = lax.all_to_all(left_parts, ("x", "y"), split_axis=0, concat_axis=0, tiled=True)
    right_parts = [
        lax.ppermute(part, "z", ring(NZ, k)) if k else part for k, part in enumerate(right_parts)
    ]
    from_right = lax.ppermute(combine_right(right_parts), ("z", "y"), home())
    action = combine(left_parts, from_right)
    action_other = lax.ppermute(action, "core", ring(2, 1))

    slab_action, over = pl.pallas_call(
        overlap_kernel,
        out_shape=(
            jax.ShapeDtypeStruct((512, 128), f32),
            jax.ShapeDtypeStruct((2 * COUPLES, 128), f32),
        ),
        in_specs=smem_specs(1) + vmem_specs(3),
        out_specs=tuple(vmem_specs(2)),
        scratch_shapes=[pltpu.VMEM((COUPLES, 8, 128), f32)] * 2,
        name="overlap",
    )(ids, action, action_other, phi_all)
    out = pl.pallas_call(
        project_kernel,
        out_shape=jax.ShapeDtypeStruct((512, 128), f32),
        in_specs=vmem_specs(2 + NY),
        out_specs=vmem_specs(1)[0],
        scratch_shapes=[pltpu.VMEM((2, COUPLES, 128), f32)],
        name="project",
    )(slab_action, phi_all, *over_y(over + lax.ppermute(over, "core", ring(2, 1))))
    return out.reshape(1, 8, G, 128)


def solution(mesh):
    grid = Mesh(mesh.devices.reshape(NZ, NX, NY, 2), ("z", "x", "y", "core"))
    placed = (P(("z", "x"), ("y", "core"), None, None), P(("z", "x"), None))
    return jax.shard_map(
        local,
        mesh=grid,
        in_specs=placed,
        out_specs=P(("z", "x"), ("y", "core"), None, None),
        check_vma=False,
    )
```

```python
import math

import jax
import jax.numpy as jnp
import ml_dtypes
import numpy as np
from jax import lax
from jax.experimental import pallas as pl
from jax.experimental.pallas import tpu as pltpu
from jax.sharding import Mesh
from jax.sharding import PartitionSpec as P

G = 64
ROWS = 2048
CHUNK = 256
KY_STEP = 32
NZ, NX, NY = 8, 4, 4
UNROLL = (8, 2, 8)
COUPLES = 32
CELLS = G * G * G
CODES = 64
FULL = 32500.0
exchange_fraction = 0.25
cell_ratio = 8.0
f32, bf16 = jnp.float32, jnp.bfloat16


def split_np(mat):
    high = mat.astype(ml_dtypes.bfloat16)
    low = (mat - high.astype(np.float64)).astype(ml_dtypes.bfloat16)
    return high, low


def plane_order():
    r = np.arange(32)
    return [16 * (r // 8) + 8 * h + r % 8 for h in (0, 1)]


def weights():
    idx = np.arange(G)
    angles = 2.0 * np.pi / G * (idx[:, None] * idx[None, :] % G)
    hart = (np.cos(angles) + np.sin(angles)) / math.sqrt(G)
    high, low = split_np(np.kron(np.eye(2), hart))
    zero = np.zeros_like(high)
    w_depth = np.block([[high, low], [high, zero]])
    w_rows = np.block([[high, high], [low, zero]])
    order = np.concatenate(plane_order())
    high, low = split_np(hart[np.ix_(order, order)])
    w_planes = np.block([[high, high], [low, np.zeros_like(high)]])
    return w_depth, w_rows, w_planes


def coulomb():
    def folded(v):
        return jnp.minimum(v, G - v).astype(f32)

    pair = lax.broadcasted_iota(jnp.int32, (G // 2, G, 128), 0)
    row = lax.broadcasted_iota(jnp.int32, (G // 2, G, 128), 1)
    lane = lax.broadcasted_iota(jnp.int32, (G // 2, G, 128), 2)
    ky = folded(2 * pair + lane // G)
    kx = cell_ratio * folded(16 * (row % 32 // 8) + 8 * (row // 32) + row % 8)
    kz = folded(lane % G)
    scale = (2.0 * math.pi / G) * (2.0 * math.pi / G)
    squared = scale * (kx * kx + ky * ky + kz * kz)
    safe = jnp.where(squared > 0, squared, 1.0)
    return jnp.where(squared > 0, -exchange_fraction / safe, 0.0)


def packed_slots(m, n, flip):
    mz, mx, nz, nx = m >> 2, m & 3, n >> 2, n & 3
    shared = 8 * flip + 16 * (m == n).astype(jnp.int32)
    first = (mz * 16 + nx * 4 + (nz >> 1)) | (mx + 4 * (nz & 1) + shared) << 7
    second = (nz * 16 + mx * 4 + (mz >> 1)) | (nx + 4 * (mz & 1) + shared) << 7
    return jnp.where(m >= 0, first | second << 16, -1)


def assign_kernel(me_ref, slots_ref, out_ref, load_ref):
    me = me_ref[0]

    def clear(i, carry):
        load_ref[i] = 0
        return carry

    lax.fori_loop(0, NZ * NX * NY, clear, 0, unroll=8)

    def one_block(b, count):
        def step(state):
            s, slot, cnt = state
            first = slot & 127
            second = (slot >> 16) & 127
            load_a = load_ref[first]
            load_b = load_ref[second]
            use_a = load_a <= load_b
            chip = jnp.where(use_a, first, second)
            load_ref[chip] = jnp.minimum(load_a, load_b) + 1
            out_ref[1 + cnt] = jnp.where(use_a, slot >> 7, slot >> 23) & 31
            slot = jnp.where(s < 31, slots_ref[b, jnp.minimum(s + 1, 31)], -1)
            return s + 1, slot, cnt + (chip == me).astype(jnp.int32)

        return lax.while_loop(lambda state: state[1] >= 0, step, (0, slots_ref[b, 0], count))[2]

    out_ref[0] = lax.fori_loop(0, 32, one_block, 0)


def split(value):
    high = value.astype(bf16)
    return high, (value - high.astype(f32)).astype(bf16)


def depth_transform(value, w_depth):
    high, low = split(value)
    out = jnp.dot(jnp.concatenate([high, low], axis=1), w_depth, preferred_element_type=f32)
    return out[:, :128] + out[:, 128:]


def rows_transform(value, w_rows):
    high, low = split(value)
    half = CHUNK // 2
    top = jnp.concatenate([high[:half], high[half:]], axis=1)
    bottom = jnp.concatenate([low[:half], low[half:]], axis=1)
    out = jnp.dot(w_rows, jnp.concatenate([top, bottom], axis=0), preferred_element_type=f32)
    out = out[:half] + out[half:]
    return jnp.concatenate([out[:, :128], out[:, 128:]], axis=0)


def planes_transform(value, w_planes):
    high, low = split(value)
    out = jnp.dot(w_planes, jnp.concatenate([high, low], axis=0), preferred_element_type=f32)
    return out[:G] + out[G:]


def gather_planes(t_ref, first, low_lanes):
    tops, bottoms = [], []
    for base in range(0, KY_STEP, 8):
        block = jnp.concatenate(
            [t_ref[pl.ds(pl.multiple_of(r * G + first + base, 8), 8)][None] for r in range(32)], axis=0
        )
        block = jnp.swapaxes(block, 0, 1)
        for p in range(0, 8, 2):
            tops.append(jnp.where(low_lanes, block[p], pltpu.roll(block[p + 1], G, 1)))
            bottoms.append(jnp.where(low_lanes, pltpu.roll(block[p], G, 1), block[p + 1]))
    return jnp.concatenate([jnp.concatenate(tops, axis=1), jnp.concatenate(bottoms, axis=1)], axis=0)


def scatter_planes(t_ref, first, value, low_lanes):
    for base in range(0, KY_STEP, 8):
        rows = []
        for p in range(base // 2, base // 2 + 4):
            top = value[:32, p * 128 : (p + 1) * 128]
            bottom = value[32:, p * 128 : (p + 1) * 128]
            rows.append(jnp.where(low_lanes, top, pltpu.roll(bottom, G, 1))[None])
            rows.append(jnp.where(low_lanes, pltpu.roll(top, G, 1), bottom)[None])
        block = jnp.swapaxes(jnp.concatenate(rows, axis=0), 0, 1)
        for r in range(32):
            t_ref[pl.ds(pl.multiple_of(r * G + first + base, 8), 8)] = block[r]


def quantize_piece(value_of, write):
    codes = []
    for p in range(8):
        rows = pl.ds(p * G, G)
        value = value_of(p)
        largest = jnp.max(jnp.abs(value), axis=0, keepdims=True)
        code = jnp.ceil(jnp.log2(jnp.maximum(largest, 1e-30)) * CODES)
        codes.append(code)
        value = jnp.round(value * (jnp.exp2(code * (-1.0 / CODES)) * FULL))
        write(rows, value.astype(jnp.int32).astype(jnp.int16))
    codes = jnp.concatenate(codes + [jnp.zeros((8, 128), f32)], axis=0)
    write(pl.ds(512, 16), codes.astype(jnp.int32).astype(jnp.int16))


def pairs_kernel(
    ids_ref,
    tasks_ref,
    left_ref,
    mine0_ref,
    mine1_ref,
    mine2_ref,
    mine3_ref,
    other0_ref,
    other1_ref,
    other2_ref,
    other3_ref,
    wz_ref,
    wy_ref,
    wx_ref,
    kern_ref,
    left_out_ref,
    sacc_ref,
    cacc_ref,
    t_ref,
    same_ref,
    cross_ref,
    lacc_ref,
):
    def clear(i, carry):
        rows = pl.ds(pl.multiple_of(i * CHUNK, CHUNK), CHUNK)
        for k in range(4):
            lacc_ref[k, rows] = jnp.zeros((CHUNK, 128), f32)
        for k in range(2):
            sacc_ref[k, rows] = jnp.zeros((CHUNK, 128), f32)
            cacc_ref[k, rows] = jnp.zeros((CHUNK, 128), f32)
        return carry

    lax.fori_loop(0, ROWS // CHUNK, clear, 0)
    keep = (lax.broadcasted_iota(jnp.int32, (G, 128), 1) < G) == (ids_ref[0] == 0)
    mine_refs = (mine0_ref, mine1_ref, mine2_ref, mine3_ref)
    other_refs = (other0_ref, other1_ref, other2_ref, other3_ref)

    def exchange(i, carry):
        source = pl.ds(pl.multiple_of(i * G, G), G)
        for k in range(NY):
            quarter = (ids_ref[1] - k) & (NY - 1)
            rows = pl.ds(pl.multiple_of(quarter * 512 + i * G, G), G)
            for j in range(2):
                mine = mine_refs[k][j, source].astype(f32)
                other = other_refs[k][j, source].astype(f32)
                same_ref[j, rows] = jnp.where(keep, mine, pltpu.roll(other, G, 1)).astype(bf16)
                cross_ref[j, rows] = jnp.where(keep, pltpu.roll(mine, G, 1), other).astype(bf16)
        return carry

    lax.fori_loop(0, 8, exchange, 0)
    low_lanes = lax.broadcasted_iota(jnp.int32, (32, 128), 1) < G

    def run(right_ref, racc_ref, task):
        a = task & 3
        b = (task >> 2) & 1
        second = 1.0 - (task >> 4).astype(f32)

        def forward(i, c):
            rows = pl.ds(pl.multiple_of(i * CHUNK, CHUNK), CHUNK)
            rho = left_ref[a, rows].astype(f32) * right_ref[b, rows].astype(f32)
            t_ref[rows] = rows_transform(depth_transform(rho, wz_ref[...]), wy_ref[...])
            return c

        lax.fori_loop(0, ROWS // CHUNK, forward, 0, unroll=UNROLL[0])

        def middle(i, c):
            first = pl.multiple_of(i * KY_STEP, KY_STEP)
            value = gather_planes(t_ref, first, low_lanes)
            kern = jnp.concatenate(
                [kern_ref[i * (KY_STEP // 2) + j] for j in range(KY_STEP // 2)], axis=1
            )
            value = planes_transform(value, wx_ref[...]) * kern
            value = planes_transform(value, wx_ref[...])
            scatter_planes(t_ref, first, value, low_lanes)
            return c

        lax.fori_loop(0, G // KY_STEP, middle, 0, unroll=UNROLL[1])

        def backward(i, c):
            rows = pl.ds(pl.multiple_of(i * CHUNK, CHUNK), CHUNK)
            v = depth_transform(rows_transform(t_ref[rows], wy_ref[...]), wz_ref[...])
            lacc_ref[a, rows] += v * right_ref[b, rows].astype(f32)
            racc_ref[b, rows] += (v * second) * left_ref[a, rows].astype(f32)
            return c

        lax.fori_loop(0, ROWS // CHUNK, backward, 0, unroll=UNROLL[2])

    def one_task(t, carry):
        task = tasks_ref[1 + t]
        flipped = (task >> 3) & 1 == 1

        @pl.when(jnp.logical_not(flipped))
        def _():
            run(same_ref, sacc_ref, task)

        @pl.when(flipped)
        def _():
            run(cross_ref, cacc_ref, task)

        return carry

    lax.fori_loop(0, tasks_ref[0], one_task, 0)

    def quantize_left(k, carry):
        def write(rows, value):
            left_out_ref[k, rows] = value

        def value_of(p):
            return lacc_ref[k // NY, pl.ds(pl.multiple_of((k % NY) * 512 + p * G, G), G)]

        quantize_piece(value_of, write)
        return carry

    lax.fori_loop(0, NX * NY, quantize_left, 0)


def quantize_right_kernel(zy_ref, first_ref, second_ref, *out_refs):
    for k in range(NZ):
        step = (zy_ref[0] + k - 2 * zy_ref[1]) & (NZ - 1)
        piece = jnp.where((step >= 1) & (step <= NY), step + NY - 1, (NZ - step) & (NZ - 1))

        def write(rows, value):
            out_refs[k][rows] = value

        def value_of(p):
            rows = pl.ds(p * G, G)
            return first_ref[piece, rows] + second_ref[piece, rows]

        quantize_piece(value_of, write)


def piece_sum(parts):
    def read(part, rows):
        return part[rows].astype(jnp.int32).astype(f32)

    scales = [jnp.exp2(read(part, pl.ds(512, 16))[:8] * (1.0 / CODES)) * (1.0 / FULL) for part in parts]

    def value_of(p):
        total = jnp.zeros((G, 128), f32)
        for part, scale in zip(parts, scales):
            total = total + read(part, pl.ds(p * G, G)) * scale[p : p + 1]
        return total

    return value_of


def combine_kernel(left_ref, right_ref, out_ref):
    value_of = piece_sum([left_ref.at[k] for k in range(NX * NY)] + [right_ref])
    for p in range(8):
        out_ref[pl.ds(p * G, G)] = value_of(p)


def combine_right_kernel(*refs):
    value_of = piece_sum(refs[:-1])

    def write(rows, value):
        refs[-1][rows] = value

    quantize_piece(value_of, write)


def quantize_right(zy, first, second):
    return pl.pallas_call(
        quantize_right_kernel,
        out_shape=(jax.ShapeDtypeStruct((528, 128), jnp.int16),) * NZ,
        in_specs=smem_specs(1) + vmem_specs(2),
        out_specs=tuple(vmem_specs(NZ)),
        cost_estimate=pl.CostEstimate(flops=0, bytes_accessed=8 * 1000 * 1000, transcendentals=0),
        name="quantize_right",
    )(zy, first, second)


def combine(left_parts, right_part):
    return pl.pallas_call(
        combine_kernel,
        out_shape=jax.ShapeDtypeStruct((512, 128), f32),
        in_specs=vmem_specs(2),
        out_specs=vmem_specs(1)[0],
        name="combine",
    )(left_parts, right_part)


def combine_right(parts):
    return pl.pallas_call(
        combine_right_kernel,
        out_shape=jax.ShapeDtypeStruct((528, 128), jnp.int16),
        in_specs=vmem_specs(len(parts)),
        out_specs=vmem_specs(1)[0],
        cost_estimate=pl.CostEstimate(flops=0, bytes_accessed=6 * 1000 * 1000, transcendentals=0),
        name="combine_right",
    )(*parts)


def overlap_kernel(core_ref, own_ref, other_ref, phi_ref, x_ref, out_ref, same_ref, cross_ref):
    keep = (lax.broadcasted_iota(jnp.int32, (G, 128), 1) < G) == (core_ref[0] == 0)
    same_ref[...] = jnp.zeros_like(same_ref)
    cross_ref[...] = jnp.zeros_like(cross_ref)

    def rows_block(i, carry):
        rows = pl.ds(pl.multiple_of(i * G, G), G)
        value = jnp.where(keep, own_ref[rows], pltpu.roll(other_ref[rows], G, 1))
        turned = pltpu.roll(value, G, 1)
        x_ref[rows] = value
        for o in range(COUPLES):
            phi = phi_ref[o, rows].astype(f32)
            same_ref[o] += jnp.sum((phi * value).reshape(8, 8, 128), axis=0)
            cross_ref[o] += jnp.sum((phi * turned).reshape(8, 8, 128), axis=0)
        return carry

    lax.fori_loop(0, 8, rows_block, 0)
    out_ref[pl.ds(0, COUPLES)] = jnp.sum(same_ref[...], axis=1)
    out_ref[pl.ds(COUPLES, COUPLES)] = jnp.sum(cross_ref[...], axis=1)


def project_kernel(x_ref, phi_ref, over0_ref, over1_ref, over2_ref, over3_ref, out_ref, coef_ref):
    lane = lax.broadcasted_iota(jnp.int32, (COUPLES, 128), 1)
    for k in range(2):
        half = pl.ds(k * COUPLES, COUPLES)
        part = (over0_ref[half] + over2_ref[half]) + (over1_ref[half] + over3_ref[half])
        low = jnp.sum(jnp.where(lane < G, part, 0.0), axis=1, keepdims=True)
        high = jnp.sum(jnp.where(lane < G, 0.0, part), axis=1, keepdims=True)
        coef_ref[k] = jnp.where(lane < G, low, high) / CELLS

    def rows_block(i, carry):
        rows = pl.ds(pl.multiple_of(i * G, G), G)
        same = jnp.zeros((G, 128), f32)
        cross = jnp.zeros((G, 128), f32)
        for o in range(COUPLES):
            phi = phi_ref[o, rows].astype(f32)
            same = same + phi * coef_ref[0, o : o + 1]
            cross = cross + phi * coef_ref[1, o : o + 1]
        out_ref[rows] = x_ref[rows] - same - pltpu.roll(cross, G, 1)
        return carry

    lax.fori_loop(0, 8, rows_block, 0)


def vmem_specs(n):
    return [pl.BlockSpec(memory_space=pltpu.VMEM)] * n


def smem_specs(n):
    return [pl.BlockSpec(memory_space=pltpu.SMEM)] * n


def lane_exchange(mine, core):
    other = lax.ppermute(mine, "core", [(0, 1), (1, 0)])
    lane = lax.broadcasted_iota(jnp.int32, mine.shape, mine.ndim - 1)
    return jnp.where((lane < G) == (core == 0), mine, jnp.roll(other, G, axis=-1))


def home():
    pairs = []
    for z in range(NZ):
        for q in range(NY):
            y, b = z // 2, z % 2
            holder = (2 * y + (q + 1 if b else -q)) % NZ
            pairs.append((holder * NY + y, z * NY + q))
    return pairs


def ring(size, step):
    return [(i, (i + step) % size) for i in range(size)]


def over_y(value):
    return [value] + [lax.ppermute(value, "y", ring(NY, k)) for k in range(1, NY)]


def local(orbitals, pair_table):
    z, x, y, core = (lax.axis_index(a) for a in ("z", "x", "y", "core"))
    mine = orbitals[0]
    slots = packed_slots(pair_table[:, 0], pair_table[:, 1], pair_table[:, 2])
    slots = lax.all_gather(slots[None], ("z", "x"), axis=0, tiled=True)
    z_couples = lax.all_gather(mine.reshape(1, 512, 128), "z", axis=0, tiled=True)
    own = lane_exchange(mine, core)
    spread = jnp.broadcast_to(own[None], (NX * NY,) + own.shape)
    left = lax.all_to_all(spread, ("x", "y"), split_axis=0, concat_axis=0, tiled=True)

    z_couples, left, slots = lax.optimization_barrier((z_couples, left, slots))
    me = (z * 16 + x * 4 + y).astype(jnp.int32).reshape(1)
    tasks = pl.pallas_call(
        assign_kernel,
        out_shape=jax.ShapeDtypeStruct((18,), jnp.int32),
        in_specs=smem_specs(2),
        out_specs=pl.BlockSpec(memory_space=pltpu.SMEM),
        scratch_shapes=[pltpu.SMEM((NZ * NX * NY,), jnp.int32)],
        cost_estimate=pl.CostEstimate(flops=0, bytes_accessed=60 * 1000 * 1000, transcendentals=0),
        name="assign",
    )(me, slots)
    phi_all = lax.all_gather(z_couples, "x", axis=0, tiled=True)
    right = []
    for k in range(NY):
        part = lax.dynamic_slice(z_couples, (2 * ((y + k) % NY), 0, 0), (2, 512, 128))
        right.append(lax.ppermute(part, "y", ring(NY, k)) if k else part)
    *right, tasks = lax.optimization_barrier((*right, tasks))
    right_other = [lax.ppermute(part, "core", ring(2, 1)) for part in right]
    ids = jnp.stack([core, y]).astype(jnp.int32)

    w_depth, w_rows, w_planes = (jnp.asarray(w) for w in weights())
    left_parts, sacc, cacc = pl.pallas_call(
        pairs_kernel,
        out_shape=(
            jax.ShapeDtypeStruct((NX * NY, 528, 128), jnp.int16),
            jax.ShapeDtypeStruct((2, ROWS, 128), f32),
            jax.ShapeDtypeStruct((2, ROWS, 128), f32),
        ),
        in_specs=smem_specs(2) + vmem_specs(5 + 2 * NY),
        out_specs=tuple(vmem_specs(3)),
        scratch_shapes=[
            pltpu.VMEM((ROWS, 128), f32),
            pltpu.VMEM((2, ROWS, 128), bf16),
            pltpu.VMEM((2, ROWS, 128), bf16),
            pltpu.VMEM((4, ROWS, 128), f32),
        ],
        compiler_params=pltpu.CompilerParams(vmem_limit_bytes=48 * 1024 * 1024),
        cost_estimate=pl.CostEstimate(flops=0, bytes_accessed=60 * 1000 * 1000, transcendentals=0),
        name="pairs",
    )(
        ids,
        tasks,
        left.reshape(4, ROWS, 128),
        *right,
        *right_other,
        w_depth,
        w_rows,
        w_planes,
        coulomb(),
    )

    other = lax.ppermute(cacc, "core", ring(2, 1))
    right_parts = quantize_right(jnp.stack([z, y]).astype(jnp.int32), sacc.reshape(NZ, 512, 128), other.reshape(NZ, 512, 128))
    left_parts = lax.all_to_all(left_parts, ("x", "y"), split_axis=0, concat_axis=0, tiled=True)
    right_parts = [
        lax.ppermute(part, "z", ring(NZ, k)) if k else part for k, part in enumerate(right_parts)
    ]
    from_right = lax.ppermute(combine_right(right_parts), ("z", "y"), home())
    action = combine(left_parts, from_right)
    action_other = lax.ppermute(action, "core", ring(2, 1))

    slab_action, over = pl.pallas_call(
        overlap_kernel,
        out_shape=(
            jax.ShapeDtypeStruct((512, 128), f32),
            jax.ShapeDtypeStruct((2 * COUPLES, 128), f32),
        ),
        in_specs=smem_specs(1) + vmem_specs(3),
        out_specs=tuple(vmem_specs(2)),
        scratch_shapes=[pltpu.VMEM((COUPLES, 8, 128), f32)] * 2,
        name="overlap",
    )(ids, action, action_other, phi_all)
    out = pl.pallas_call(
        project_kernel,
        out_shape=jax.ShapeDtypeStruct((512, 128), f32),
        in_specs=vmem_specs(2 + NY),
        out_specs=vmem_specs(1)[0],
        scratch_shapes=[pltpu.VMEM((2, COUPLES, 128), f32)],
        name="project",
    )(slab_action, phi_all, *over_y(over + lax.ppermute(over, "core", ring(2, 1))))
    return out.reshape(1, 8, G, 128)


def solution(mesh):
    grid = Mesh(mesh.devices.reshape(NZ, NX, NY, 2), ("z", "x", "y", "core"))
    placed = (P(("z", "x"), ("y", "core"), None, None), P(("z", "x"), None))
    return jax.shard_map(
        local,
        mesh=grid,
        in_specs=placed,
        out_specs=P(("z", "x"), ("y", "core"), None, None),
        check_vma=False,
    )
```

```python
import math

import jax
import jax.numpy as jnp
import ml_dtypes
import numpy as np
from jax import lax
from jax.experimental import pallas as pl
from jax.experimental.pallas import tpu as pltpu
from jax.sharding import Mesh
from jax.sharding import PartitionSpec as P

G = 64
ROWS = 2048
CHUNK = 256
KY_STEP = 32
NZ, NX, NY = 8, 4, 4
UNROLL = (8, 2, 8)
COUPLES = 32
CELLS = G * G * G
CODES = 64
FULL = 32500.0
exchange_fraction = 0.25
cell_ratio = 8.0
f32, bf16 = jnp.float32, jnp.bfloat16


def split_np(mat):
    high = mat.astype(ml_dtypes.bfloat16)
    low = (mat - high.astype(np.float64)).astype(ml_dtypes.bfloat16)
    return high, low


def plane_order():
    r = np.arange(32)
    return [16 * (r // 8) + 8 * h + r % 8 for h in (0, 1)]


def weights():
    idx = np.arange(G)
    angles = 2.0 * np.pi / G * (idx[:, None] * idx[None, :] % G)
    hart = (np.cos(angles) + np.sin(angles)) / math.sqrt(G)
    high, low = split_np(np.kron(np.eye(2), hart))
    zero = np.zeros_like(high)
    w_depth = np.block([[high, low], [high, zero]])
    w_rows = np.block([[high, high], [low, zero]])
    order = np.concatenate(plane_order())
    high, low = split_np(hart[np.ix_(order, order)])
    w_planes = np.block([[high, high], [low, np.zeros_like(high)]])
    return w_depth, w_rows, w_planes


def coulomb():
    def folded(v):
        return jnp.minimum(v, G - v).astype(f32)

    pair = lax.broadcasted_iota(jnp.int32, (G // 2, G, 128), 0)
    row = lax.broadcasted_iota(jnp.int32, (G // 2, G, 128), 1)
    lane = lax.broadcasted_iota(jnp.int32, (G // 2, G, 128), 2)
    ky = folded(2 * pair + lane // G)
    kx = cell_ratio * folded(16 * (row % 32 // 8) + 8 * (row // 32) + row % 8)
    kz = folded(lane % G)
    scale = (2.0 * math.pi / G) * (2.0 * math.pi / G)
    squared = scale * (kx * kx + ky * ky + kz * kz)
    safe = jnp.where(squared > 0, squared, 1.0)
    return jnp.where(squared > 0, -exchange_fraction / safe, 0.0)


def packed_slots(m, n, flip):
    mz, mx, nz, nx = m >> 2, m & 3, n >> 2, n & 3
    shared = 8 * flip + 16 * (m == n).astype(jnp.int32)
    first = (mz * 16 + nx * 4 + (nz >> 1)) | (mx + 4 * (nz & 1) + shared) << 7
    second = (nz * 16 + mx * 4 + (mz >> 1)) | (nx + 4 * (mz & 1) + shared) << 7
    return jnp.where(m >= 0, first | second << 16, -1)


def assign_kernel(me_ref, slots_ref, out_ref, load_ref):
    me = me_ref[0]

    def clear(i, carry):
        load_ref[i] = 0
        return carry

    lax.fori_loop(0, NZ * NX * NY, clear, 0, unroll=8)

    def one_block(b, count):
        def step(state):
            s, slot, cnt = state
            first = slot & 127
            second = (slot >> 16) & 127
            load_a = load_ref[first]
            load_b = load_ref[second]
            use_a = load_a <= load_b
            chip = jnp.where(use_a, first, second)
            load_ref[chip] = jnp.minimum(load_a, load_b) + 1
            out_ref[1 + cnt] = jnp.where(use_a, slot >> 7, slot >> 23) & 31
            slot = jnp.where(s < 31, slots_ref[b, jnp.minimum(s + 1, 31)], -1)
            return s + 1, slot, cnt + (chip == me).astype(jnp.int32)

        return lax.while_loop(lambda state: state[1] >= 0, step, (0, slots_ref[b, 0], count))[2]

    out_ref[0] = lax.fori_loop(0, 32, one_block, 0)


def split(value):
    high = value.astype(bf16)
    return high, (value - high.astype(f32)).astype(bf16)


def depth_transform(value, w_depth):
    high, low = split(value)
    out = jnp.dot(jnp.concatenate([high, low], axis=1), w_depth, preferred_element_type=f32)
    return out[:, :128] + out[:, 128:]


def rows_transform(value, w_rows):
    high, low = split(value)
    half = CHUNK // 2
    top = jnp.concatenate([high[:half], high[half:]], axis=1)
    bottom = jnp.concatenate([low[:half], low[half:]], axis=1)
    out = jnp.dot(w_rows, jnp.concatenate([top, bottom], axis=0), preferred_element_type=f32)
    out = out[:half] + out[half:]
    return jnp.concatenate([out[:, :128], out[:, 128:]], axis=0)


def planes_transform(value, w_planes):
    high, low = split(value)
    out = jnp.dot(w_planes, jnp.concatenate([high, low], axis=0), preferred_element_type=f32)
    return out[:G] + out[G:]


def gather_planes(t_ref, first, low_lanes):
    tops, bottoms = [], []
    for base in range(0, KY_STEP, 8):
        block = jnp.concatenate(
            [t_ref[pl.ds(pl.multiple_of(r * G + first + base, 8), 8)][None] for r in range(32)], axis=0
        )
        block = jnp.swapaxes(block, 0, 1)
        for p in range(0, 8, 2):
            tops.append(jnp.where(low_lanes, block[p], pltpu.roll(block[p + 1], G, 1)))
            bottoms.append(jnp.where(low_lanes, pltpu.roll(block[p], G, 1), block[p + 1]))
    return jnp.concatenate([jnp.concatenate(tops, axis=1), jnp.concatenate(bottoms, axis=1)], axis=0)


def scatter_planes(t_ref, first, value, low_lanes):
    for base in range(0, KY_STEP, 8):
        rows = []
        for p in range(base // 2, base // 2 + 4):
            top = value[:32, p * 128 : (p + 1) * 128]
            bottom = value[32:, p * 128 : (p + 1) * 128]
            rows.append(jnp.where(low_lanes, top, pltpu.roll(bottom, G, 1))[None])
            rows.append(jnp.where(low_lanes, pltpu.roll(top, G, 1), bottom)[None])
        block = jnp.swapaxes(jnp.concatenate(rows, axis=0), 0, 1)
        for r in range(32):
            t_ref[pl.ds(pl.multiple_of(r * G + first + base, 8), 8)] = block[r]


def quantize_piece(value_of, write):
    codes = []
    for p in range(8):
        rows = pl.ds(p * G, G)
        value = value_of(p)
        largest = jnp.max(jnp.abs(value), axis=0, keepdims=True)
        code = jnp.ceil(jnp.log2(jnp.maximum(largest, 1e-30)) * CODES)
        codes.append(code)
        value = jnp.round(value * (jnp.exp2(code * (-1.0 / CODES)) * FULL))
        write(rows, value.astype(jnp.int32).astype(jnp.int16))
    codes = jnp.concatenate(codes + [jnp.zeros((8, 128), f32)], axis=0)
    write(pl.ds(512, 16), codes.astype(jnp.int32).astype(jnp.int16))


def pairs_kernel(
    ids_ref,
    tasks_ref,
    left_ref,
    mine0_ref,
    mine1_ref,
    mine2_ref,
    mine3_ref,
    other0_ref,
    other1_ref,
    other2_ref,
    other3_ref,
    wz_ref,
    wy_ref,
    wx_ref,
    kern_ref,
    left_out_ref,
    sacc_ref,
    cacc_ref,
    t_ref,
    same_ref,
    cross_ref,
    lacc_ref,
):
    def clear(i, carry):
        rows = pl.ds(pl.multiple_of(i * CHUNK, CHUNK), CHUNK)
        for k in range(4):
            lacc_ref[k, rows] = jnp.zeros((CHUNK, 128), f32)
        for k in range(2):
            sacc_ref[k, rows] = jnp.zeros((CHUNK, 128), f32)
            cacc_ref[k, rows] = jnp.zeros((CHUNK, 128), f32)
        return carry

    lax.fori_loop(0, ROWS // CHUNK, clear, 0)
    keep = (lax.broadcasted_iota(jnp.int32, (G, 128), 1) < G) == (ids_ref[0] == 0)
    mine_refs = (mine0_ref, mine1_ref, mine2_ref, mine3_ref)
    other_refs = (other0_ref, other1_ref, other2_ref, other3_ref)

    def exchange(i, carry):
        source = pl.ds(pl.multiple_of(i * G, G), G)
        for k in range(NY):
            quarter = (ids_ref[1] - k) & (NY - 1)
            rows = pl.ds(pl.multiple_of(quarter * 512 + i * G, G), G)
            for j in range(2):
                mine = mine_refs[k][j, source].astype(f32)
                other = other_refs[k][j, source].astype(f32)
                same_ref[j, rows] = jnp.where(keep, mine, pltpu.roll(other, G, 1)).astype(bf16)
                cross_ref[j, rows] = jnp.where(keep, pltpu.roll(mine, G, 1), other).astype(bf16)
        return carry

    lax.fori_loop(0, 8, exchange, 0)
    low_lanes = lax.broadcasted_iota(jnp.int32, (32, 128), 1) < G

    def run(right_ref, racc_ref, task):
        a = task & 3
        b = (task >> 2) & 1
        second = 1.0 - (task >> 4).astype(f32)

        def forward(i, c):
            rows = pl.ds(pl.multiple_of(i * CHUNK, CHUNK), CHUNK)
            rho = left_ref[a, rows].astype(f32) * right_ref[b, rows].astype(f32)
            t_ref[rows] = rows_transform(depth_transform(rho, wz_ref[...]), wy_ref[...])
            return c

        lax.fori_loop(0, ROWS // CHUNK, forward, 0, unroll=UNROLL[0])

        def middle(i, c):
            first = pl.multiple_of(i * KY_STEP, KY_STEP)
            value = gather_planes(t_ref, first, low_lanes)
            kern = jnp.concatenate(
                [kern_ref[i * (KY_STEP // 2) + j] for j in range(KY_STEP // 2)], axis=1
            )
            value = planes_transform(value, wx_ref[...]) * kern
            value = planes_transform(value, wx_ref[...])
            scatter_planes(t_ref, first, value, low_lanes)
            return c

        lax.fori_loop(0, G // KY_STEP, middle, 0, unroll=UNROLL[1])

        def backward(i, c):
            rows = pl.ds(pl.multiple_of(i * CHUNK, CHUNK), CHUNK)
            v = depth_transform(rows_transform(t_ref[rows], wy_ref[...]), wz_ref[...])
            lacc_ref[a, rows] += v * right_ref[b, rows].astype(f32)
            racc_ref[b, rows] += (v * second) * left_ref[a, rows].astype(f32)
            return c

        lax.fori_loop(0, ROWS // CHUNK, backward, 0, unroll=UNROLL[2])

    def one_task(t, carry):
        task = tasks_ref[1 + t]
        flipped = (task >> 3) & 1 == 1

        @pl.when(jnp.logical_not(flipped))
        def _():
            run(same_ref, sacc_ref, task)

        @pl.when(flipped)
        def _():
            run(cross_ref, cacc_ref, task)

        return carry

    lax.fori_loop(0, tasks_ref[0], one_task, 0)

    def quantize_left(k, carry):
        def write(rows, value):
            left_out_ref[k, rows] = value

        def value_of(p):
            return lacc_ref[k // NY, pl.ds(pl.multiple_of((k % NY) * 512 + p * G, G), G)]

        quantize_piece(value_of, write)
        return carry

    lax.fori_loop(0, NX * NY, quantize_left, 0)


def quantize_right_kernel(zy_ref, first_ref, second_ref, *out_refs):
    for k in range(NZ):
        step = (zy_ref[0] + k - 2 * zy_ref[1]) & (NZ - 1)
        piece = jnp.where((step >= 1) & (step <= NY), step + NY - 1, (NZ - step) & (NZ - 1))

        def write(rows, value):
            out_refs[k][rows] = value

        def value_of(p):
            rows = pl.ds(p * G, G)
            return first_ref[piece, rows] + second_ref[piece, rows]

        quantize_piece(value_of, write)


def piece_sum(parts):
    def read(part, rows):
        return part[rows].astype(jnp.int32).astype(f32)

    scales = [jnp.exp2(read(part, pl.ds(512, 16))[:8] * (1.0 / CODES)) * (1.0 / FULL) for part in parts]

    def value_of(p):
        total = jnp.zeros((G, 128), f32)
        for part, scale in zip(parts, scales):
            total = total + read(part, pl.ds(p * G, G)) * scale[p : p + 1]
        return total

    return value_of


def combine_kernel(left_ref, right_ref, out_ref):
    value_of = piece_sum([left_ref.at[k] for k in range(NX * NY)] + [right_ref])
    for p in range(8):
        out_ref[pl.ds(p * G, G)] = value_of(p)


def combine_right_kernel(*refs):
    value_of = piece_sum(refs[:-1])

    def write(rows, value):
        refs[-1][rows] = value

    quantize_piece(value_of, write)


def quantize_right(zy, first, second):
    return pl.pallas_call(
        quantize_right_kernel,
        out_shape=(jax.ShapeDtypeStruct((528, 128), jnp.int16),) * NZ,
        in_specs=smem_specs(1) + vmem_specs(2),
        out_specs=tuple(vmem_specs(NZ)),
        cost_estimate=pl.CostEstimate(flops=0, bytes_accessed=8 * 1000 * 1000, transcendentals=0),
        name="quantize_right",
    )(zy, first, second)


def combine(left_parts, right_part):
    return pl.pallas_call(
        combine_kernel,
        out_shape=jax.ShapeDtypeStruct((512, 128), f32),
        in_specs=vmem_specs(2),
        out_specs=vmem_specs(1)[0],
        name="combine",
    )(left_parts, right_part)


def combine_right(parts):
    return pl.pallas_call(
        combine_right_kernel,
        out_shape=jax.ShapeDtypeStruct((528, 128), jnp.int16),
        in_specs=vmem_specs(len(parts)),
        out_specs=vmem_specs(1)[0],
        cost_estimate=pl.CostEstimate(flops=0, bytes_accessed=6 * 1000 * 1000, transcendentals=0),
        name="combine_right",
    )(*parts)


def overlap_kernel(core_ref, own_ref, other_ref, phi_ref, x_ref, out_ref, same_ref, cross_ref):
    keep = (lax.broadcasted_iota(jnp.int32, (G, 128), 1) < G) == (core_ref[0] == 0)
    same_ref[...] = jnp.zeros_like(same_ref)
    cross_ref[...] = jnp.zeros_like(cross_ref)

    def rows_block(i, carry):
        rows = pl.ds(pl.multiple_of(i * G, G), G)
        value = jnp.where(keep, own_ref[rows], pltpu.roll(other_ref[rows], G, 1))
        turned = pltpu.roll(value, G, 1)
        x_ref[rows] = value
        for o in range(COUPLES):
            phi = phi_ref[o, rows].astype(f32)
            same_ref[o] += jnp.sum((phi * value).reshape(8, 8, 128), axis=0)
            cross_ref[o] += jnp.sum((phi * turned).reshape(8, 8, 128), axis=0)
        return carry

    lax.fori_loop(0, 8, rows_block, 0)
    out_ref[pl.ds(0, COUPLES)] = jnp.sum(same_ref[...], axis=1)
    out_ref[pl.ds(COUPLES, COUPLES)] = jnp.sum(cross_ref[...], axis=1)


def project_kernel(x_ref, phi_ref, over0_ref, over1_ref, over2_ref, over3_ref, out_ref, coef_ref):
    lane = lax.broadcasted_iota(jnp.int32, (COUPLES, 128), 1)
    for k in range(2):
        half = pl.ds(k * COUPLES, COUPLES)
        part = (over0_ref[half] + over2_ref[half]) + (over1_ref[half] + over3_ref[half])
        low = jnp.sum(jnp.where(lane < G, part, 0.0), axis=1, keepdims=True)
        high = jnp.sum(jnp.where(lane < G, 0.0, part), axis=1, keepdims=True)
        coef_ref[k] = jnp.where(lane < G, low, high) / CELLS

    def rows_block(i, carry):
        rows = pl.ds(pl.multiple_of(i * G, G), G)
        same = jnp.zeros((G, 128), f32)
        cross = jnp.zeros((G, 128), f32)
        for o in range(COUPLES):
            phi = phi_ref[o, rows].astype(f32)
            same = same + phi * coef_ref[0, o : o + 1]
            cross = cross + phi * coef_ref[1, o : o + 1]
        out_ref[rows] = x_ref[rows] - same - pltpu.roll(cross, G, 1)
        return carry

    lax.fori_loop(0, 8, rows_block, 0)


def vmem_specs(n):
    return [pl.BlockSpec(memory_space=pltpu.VMEM)] * n


def smem_specs(n):
    return [pl.BlockSpec(memory_space=pltpu.SMEM)] * n


def lane_exchange(mine, core):
    other = lax.ppermute(mine, "core", [(0, 1), (1, 0)])
    lane = lax.broadcasted_iota(jnp.int32, mine.shape, mine.ndim - 1)
    return jnp.where((lane < G) == (core == 0), mine, jnp.roll(other, G, axis=-1))


def home():
    pairs = []
    for z in range(NZ):
        for q in range(NY):
            y, b = z // 2, z % 2
            holder = (2 * y + (q + 1 if b else -q)) % NZ
            pairs.append((holder * NY + y, z * NY + q))
    return pairs


def ring(size, step):
    return [(i, (i + step) % size) for i in range(size)]


def over_y(value):
    return [value] + [lax.ppermute(value, "y", ring(NY, k)) for k in range(1, NY)]


def local(orbitals, pair_table):
    z, x, y, core = (lax.axis_index(a) for a in ("z", "x", "y", "core"))
    mine = orbitals[0]
    slots = packed_slots(pair_table[:, 0], pair_table[:, 1], pair_table[:, 2])
    slots = lax.all_gather(slots[None], ("z", "x"), axis=0, tiled=True)
    z_couples = lax.all_gather(mine.reshape(1, 512, 128), "z", axis=0, tiled=True)
    own = lane_exchange(mine, core)
    own, slots = lax.optimization_barrier((own, slots))
    spread = jnp.broadcast_to(own[None], (NX * NY,) + own.shape)
    left = lax.all_to_all(spread, ("x", "y"), split_axis=0, concat_axis=0, tiled=True)

    me = (z * 16 + x * 4 + y).astype(jnp.int32).reshape(1)
    tasks = pl.pallas_call(
        assign_kernel,
        out_shape=jax.ShapeDtypeStruct((18,), jnp.int32),
        in_specs=smem_specs(2),
        out_specs=pl.BlockSpec(memory_space=pltpu.SMEM),
        scratch_shapes=[pltpu.SMEM((NZ * NX * NY,), jnp.int32)],
        cost_estimate=pl.CostEstimate(flops=0, bytes_accessed=60 * 1000 * 1000, transcendentals=0),
        name="assign",
    )(me, slots)
    z_couples, tasks = lax.optimization_barrier((z_couples, tasks))
    phi_all = lax.all_gather(z_couples, "x", axis=0, tiled=True)
    right = []
    for k in range(NY):
        part = lax.dynamic_slice(z_couples, (2 * ((y + k) % NY), 0, 0), (2, 512, 128))
        right.append(lax.ppermute(part, "y", ring(NY, k)) if k else part)
    right_other = [lax.ppermute(part, "core", ring(2, 1)) for part in right]
    ids = jnp.stack([core, y]).astype(jnp.int32)

    w_depth, w_rows, w_planes = (jnp.asarray(w) for w in weights())
    left_parts, sacc, cacc = pl.pallas_call(
        pairs_kernel,
        out_shape=(
            jax.ShapeDtypeStruct((NX * NY, 528, 128), jnp.int16),
            jax.ShapeDtypeStruct((2, ROWS, 128), f32),
            jax.ShapeDtypeStruct((2, ROWS, 128), f32),
        ),
        in_specs=smem_specs(2) + vmem_specs(5 + 2 * NY),
        out_specs=tuple(vmem_specs(3)),
        scratch_shapes=[
            pltpu.VMEM((ROWS, 128), f32),
            pltpu.VMEM((2, ROWS, 128), bf16),
            pltpu.VMEM((2, ROWS, 128), bf16),
            pltpu.VMEM((4, ROWS, 128), f32),
        ],
        compiler_params=pltpu.CompilerParams(vmem_limit_bytes=48 * 1024 * 1024),
        cost_estimate=pl.CostEstimate(flops=0, bytes_accessed=60 * 1000 * 1000, transcendentals=0),
        name="pairs",
    )(
        ids,
        tasks,
        left.reshape(4, ROWS, 128),
        *right,
        *right_other,
        w_depth,
        w_rows,
        w_planes,
        coulomb(),
    )

    other = lax.ppermute(cacc, "core", ring(2, 1))
    right_parts = quantize_right(jnp.stack([z, y]).astype(jnp.int32), sacc.reshape(NZ, 512, 128), other.reshape(NZ, 512, 128))
    left_parts = lax.all_to_all(left_parts, ("x", "y"), split_axis=0, concat_axis=0, tiled=True)
    right_parts = [
        lax.ppermute(part, "z", ring(NZ, k)) if k else part for k, part in enumerate(right_parts)
    ]
    from_right = lax.ppermute(combine_right(right_parts), ("z", "y"), home())
    action = combine(left_parts, from_right)
    action_other = lax.ppermute(action, "core", ring(2, 1))

    slab_action, over = pl.pallas_call(
        overlap_kernel,
        out_shape=(
            jax.ShapeDtypeStruct((512, 128), f32),
            jax.ShapeDtypeStruct((2 * COUPLES, 128), f32),
        ),
        in_specs=smem_specs(1) + vmem_specs(3),
        out_specs=tuple(vmem_specs(2)),
        scratch_shapes=[pltpu.VMEM((COUPLES, 8, 128), f32)] * 2,
        name="overlap",
    )(ids, action, action_other, phi_all)
    out = pl.pallas_call(
        project_kernel,
        out_shape=jax.ShapeDtypeStruct((512, 128), f32),
        in_specs=vmem_specs(2 + NY),
        out_specs=vmem_specs(1)[0],
        scratch_shapes=[pltpu.VMEM((2, COUPLES, 128), f32)],
        name="project",
    )(slab_action, phi_all, *over_y(over + lax.ppermute(over, "core", ring(2, 1))))
    return out.reshape(1, 8, G, 128)


def solution(mesh):
    grid = Mesh(mesh.devices.reshape(NZ, NX, NY, 2), ("z", "x", "y", "core"))
    placed = (P(("z", "x"), ("y", "core"), None, None), P(("z", "x"), None))
    return jax.shard_map(
        local,
        mesh=grid,
        in_specs=placed,
        out_specs=P(("z", "x"), ("y", "core"), None, None),
        check_vma=False,
    )
```

```python
import math

import jax
import jax.numpy as jnp
import ml_dtypes
import numpy as np
from jax import lax
from jax.experimental import pallas as pl
from jax.experimental.pallas import tpu as pltpu
from jax.sharding import Mesh
from jax.sharding import PartitionSpec as P

G = 64
ROWS = 2048
CHUNK = 256
KY_STEP = 32
NZ, NX, NY = 8, 4, 4
UNROLL = (8, 2, 8)
COUPLES = 32
CELLS = G * G * G
CODES = 64
FULL = 32500.0
exchange_fraction = 0.25
cell_ratio = 8.0
f32, bf16 = jnp.float32, jnp.bfloat16


def split_np(mat):
    high = mat.astype(ml_dtypes.bfloat16)
    low = (mat - high.astype(np.float64)).astype(ml_dtypes.bfloat16)
    return high, low


def plane_order():
    r = np.arange(32)
    return [16 * (r // 8) + 8 * h + r % 8 for h in (0, 1)]


def weights():
    idx = np.arange(G)
    angles = 2.0 * np.pi / G * (idx[:, None] * idx[None, :] % G)
    hart = (np.cos(angles) + np.sin(angles)) / math.sqrt(G)
    high, low = split_np(np.kron(np.eye(2), hart))
    zero = np.zeros_like(high)
    w_depth = np.block([[high, low], [high, zero]])
    w_rows = np.block([[high, high], [low, zero]])
    order = np.concatenate(plane_order())
    high, low = split_np(hart[np.ix_(order, order)])
    w_planes = np.block([[high, high], [low, np.zeros_like(high)]])
    return w_depth, w_rows, w_planes


def coulomb():
    def folded(v):
        return jnp.minimum(v, G - v).astype(f32)

    pair = lax.broadcasted_iota(jnp.int32, (G // 2, G, 128), 0)
    row = lax.broadcasted_iota(jnp.int32, (G // 2, G, 128), 1)
    lane = lax.broadcasted_iota(jnp.int32, (G // 2, G, 128), 2)
    ky = folded(2 * pair + lane // G)
    kx = cell_ratio * folded(16 * (row % 32 // 8) + 8 * (row // 32) + row % 8)
    kz = folded(lane % G)
    scale = (2.0 * math.pi / G) * (2.0 * math.pi / G)
    squared = scale * (kx * kx + ky * ky + kz * kz)
    safe = jnp.where(squared > 0, squared, 1.0)
    return jnp.where(squared > 0, -exchange_fraction / safe, 0.0)


def packed_slots(m, n, flip):
    mz, mx, nz, nx = m >> 2, m & 3, n >> 2, n & 3
    shared = 8 * flip + 16 * (m == n).astype(jnp.int32)
    first = (mz * 16 + nx * 4 + (nz >> 1)) | (mx + 4 * (nz & 1) + shared) << 7
    second = (nz * 16 + mx * 4 + (mz >> 1)) | (nx + 4 * (mz & 1) + shared) << 7
    return jnp.where(m >= 0, first | second << 16, -1)


def assign_kernel(me_ref, slots_ref, out_ref, load_ref):
    me = me_ref[0]

    def clear(i, carry):
        load_ref[i] = 0
        return carry

    lax.fori_loop(0, NZ * NX * NY, clear, 0, unroll=8)

    def one_block(b, count):
        def step(state):
            s, slot, cnt = state
            first = slot & 127
            second = (slot >> 16) & 127
            load_a = load_ref[first]
            load_b = load_ref[second]
            use_a = load_a <= load_b
            chip = jnp.where(use_a, first, second)
            load_ref[chip] = jnp.minimum(load_a, load_b) + 1
            out_ref[1 + cnt] = jnp.where(use_a, slot >> 7, slot >> 23) & 31
            slot = jnp.where(s < 31, slots_ref[b, jnp.minimum(s + 1, 31)], -1)
            return s + 1, slot, cnt + (chip == me).astype(jnp.int32)

        return lax.while_loop(lambda state: state[1] >= 0, step, (0, slots_ref[b, 0], count))[2]

    out_ref[0] = lax.fori_loop(0, 32, one_block, 0)


def split(value):
    high = value.astype(bf16)
    return high, (value - high.astype(f32)).astype(bf16)


def depth_transform(value, w_depth):
    high, low = split(value)
    out = jnp.dot(jnp.concatenate([high, low], axis=1), w_depth, preferred_element_type=f32)
    return out[:, :128] + out[:, 128:]


def rows_transform(value, w_rows):
    high, low = split(value)
    half = CHUNK // 2
    top = jnp.concatenate([high[:half], high[half:]], axis=1)
    bottom = jnp.concatenate([low[:half], low[half:]], axis=1)
    out = jnp.dot(w_rows, jnp.concatenate([top, bottom], axis=0), preferred_element_type=f32)
    out = out[:half] + out[half:]
    return jnp.concatenate([out[:, :128], out[:, 128:]], axis=0)


def planes_transform(value, w_planes):
    high, low = split(value)
    out = jnp.dot(w_planes, jnp.concatenate([high, low], axis=0), preferred_element_type=f32)
    return out[:G] + out[G:]


def gather_planes(t_ref, first, low_lanes):
    tops, bottoms = [], []
    for base in range(0, KY_STEP, 8):
        block = jnp.concatenate(
            [t_ref[pl.ds(pl.multiple_of(r * G + first + base, 8), 8)][None] for r in range(32)], axis=0
        )
        block = jnp.swapaxes(block, 0, 1)
        for p in range(0, 8, 2):
            tops.append(jnp.where(low_lanes, block[p], pltpu.roll(block[p + 1], G, 1)))
            bottoms.append(jnp.where(low_lanes, pltpu.roll(block[p], G, 1), block[p + 1]))
    return jnp.concatenate([jnp.concatenate(tops, axis=1), jnp.concatenate(bottoms, axis=1)], axis=0)


def scatter_planes(t_ref, first, value, low_lanes):
    for base in range(0, KY_STEP, 8):
        rows = []
        for p in range(base // 2, base // 2 + 4):
            top = value[:32, p * 128 : (p + 1) * 128]
            bottom = value[32:, p * 128 : (p + 1) * 128]
            rows.append(jnp.where(low_lanes, top, pltpu.roll(bottom, G, 1))[None])
            rows.append(jnp.where(low_lanes, pltpu.roll(top, G, 1), bottom)[None])
        block = jnp.swapaxes(jnp.concatenate(rows, axis=0), 0, 1)
        for r in range(32):
            t_ref[pl.ds(pl.multiple_of(r * G + first + base, 8), 8)] = block[r]


def quantize_piece(value_of, write):
    codes = []
    for p in range(8):
        rows = pl.ds(p * G, G)
        value = value_of(p)
        largest = jnp.max(jnp.abs(value), axis=0, keepdims=True)
        code = jnp.ceil(jnp.log2(jnp.maximum(largest, 1e-30)) * CODES)
        codes.append(code)
        value = jnp.round(value * (jnp.exp2(code * (-1.0 / CODES)) * FULL))
        write(rows, value.astype(jnp.int32).astype(jnp.int16))
    codes = jnp.concatenate(codes + [jnp.zeros((8, 128), f32)], axis=0)
    write(pl.ds(512, 16), codes.astype(jnp.int32).astype(jnp.int16))


def pairs_kernel(
    ids_ref,
    tasks_ref,
    left_ref,
    mine_ref,
    other_ref,
    wz_ref,
    wy_ref,
    wx_ref,
    kern_ref,
    left_out_ref,
    sacc_ref,
    cacc_ref,
    t_ref,
    same_ref,
    cross_ref,
    lacc_ref,
):
    def clear(i, carry):
        rows = pl.ds(pl.multiple_of(i * CHUNK, CHUNK), CHUNK)
        for k in range(4):
            lacc_ref[k, rows] = jnp.zeros((CHUNK, 128), f32)
        for k in range(2):
            sacc_ref[k, rows] = jnp.zeros((CHUNK, 128), f32)
            cacc_ref[k, rows] = jnp.zeros((CHUNK, 128), f32)
        return carry

    lax.fori_loop(0, ROWS // CHUNK, clear, 0)
    keep = (lax.broadcasted_iota(jnp.int32, (G, 128), 1) < G) == (ids_ref[0] == 0)

    def exchange(i, carry):
        source = pl.ds(pl.multiple_of(i * G, G), G)
        for quarter in range(NY):
            rows = pl.ds(pl.multiple_of(quarter * 512 + i * G, G), G)
            for j in range(2):
                mine = mine_ref[2 * quarter + j, source].astype(f32)
                other = other_ref[2 * quarter + j, source].astype(f32)
                same_ref[j, rows] = jnp.where(keep, mine, pltpu.roll(other, G, 1)).astype(bf16)
                cross_ref[j, rows] = jnp.where(keep, pltpu.roll(mine, G, 1), other).astype(bf16)
        return carry

    lax.fori_loop(0, 8, exchange, 0)
    low_lanes = lax.broadcasted_iota(jnp.int32, (32, 128), 1) < G

    def run(right_ref, racc_ref, task):
        a = task & 3
        b = (task >> 2) & 1
        second = 1.0 - (task >> 4).astype(f32)

        def forward(i, c):
            rows = pl.ds(pl.multiple_of(i * CHUNK, CHUNK), CHUNK)
            rho = left_ref[a, rows].astype(f32) * right_ref[b, rows].astype(f32)
            t_ref[rows] = rows_transform(depth_transform(rho, wz_ref[...]), wy_ref[...])
            return c

        lax.fori_loop(0, ROWS // CHUNK, forward, 0, unroll=UNROLL[0])

        def middle(i, c):
            first = pl.multiple_of(i * KY_STEP, KY_STEP)
            value = gather_planes(t_ref, first, low_lanes)
            kern = jnp.concatenate(
                [kern_ref[i * (KY_STEP // 2) + j] for j in range(KY_STEP // 2)], axis=1
            )
            value = planes_transform(value, wx_ref[...]) * kern
            value = planes_transform(value, wx_ref[...])
            scatter_planes(t_ref, first, value, low_lanes)
            return c

        lax.fori_loop(0, G // KY_STEP, middle, 0, unroll=UNROLL[1])

        def backward(i, c):
            rows = pl.ds(pl.multiple_of(i * CHUNK, CHUNK), CHUNK)
            v = depth_transform(rows_transform(t_ref[rows], wy_ref[...]), wz_ref[...])
            lacc_ref[a, rows] += v * right_ref[b, rows].astype(f32)
            racc_ref[b, rows] += (v * second) * left_ref[a, rows].astype(f32)
            return c

        lax.fori_loop(0, ROWS // CHUNK, backward, 0, unroll=UNROLL[2])

    def one_task(t, carry):
        task = tasks_ref[1 + t]
        flipped = (task >> 3) & 1 == 1

        @pl.when(jnp.logical_not(flipped))
        def _():
            run(same_ref, sacc_ref, task)

        @pl.when(flipped)
        def _():
            run(cross_ref, cacc_ref, task)

        return carry

    lax.fori_loop(0, tasks_ref[0], one_task, 0)

    def quantize_left(k, carry):
        def write(rows, value):
            left_out_ref[k, rows] = value

        def value_of(p):
            return lacc_ref[k // NY, pl.ds(pl.multiple_of((k % NY) * 512 + p * G, G), G)]

        quantize_piece(value_of, write)
        return carry

    lax.fori_loop(0, NX * NY, quantize_left, 0)


def quantize_right_kernel(zy_ref, first_ref, second_ref, *out_refs):
    for k in range(NZ):
        step = (zy_ref[0] + k - 2 * zy_ref[1]) & (NZ - 1)
        piece = jnp.where((step >= 1) & (step <= NY), step + NY - 1, (NZ - step) & (NZ - 1))

        def write(rows, value):
            out_refs[k][rows] = value

        def value_of(p):
            rows = pl.ds(p * G, G)
            return first_ref[piece, rows] + second_ref[piece, rows]

        quantize_piece(value_of, write)


def piece_sum(parts):
    def read(part, rows):
        return part[rows].astype(jnp.int32).astype(f32)

    scales = [jnp.exp2(read(part, pl.ds(512, 16))[:8] * (1.0 / CODES)) * (1.0 / FULL) for part in parts]

    def value_of(p):
        total = jnp.zeros((G, 128), f32)
        for part, scale in zip(parts, scales):
            total = total + read(part, pl.ds(p * G, G)) * scale[p : p + 1]
        return total

    return value_of


def combine_kernel(left_ref, right_ref, out_ref):
    value_of = piece_sum([left_ref.at[k] for k in range(NX * NY)] + [right_ref])
    for p in range(8):
        out_ref[pl.ds(p * G, G)] = value_of(p)


def combine_right_kernel(*refs):
    value_of = piece_sum(refs[:-1])

    def write(rows, value):
        refs[-1][rows] = value

    quantize_piece(value_of, write)


def quantize_right(zy, first, second):
    return pl.pallas_call(
        quantize_right_kernel,
        out_shape=(jax.ShapeDtypeStruct((528, 128), jnp.int16),) * NZ,
        in_specs=smem_specs(1) + vmem_specs(2),
        out_specs=tuple(vmem_specs(NZ)),
        cost_estimate=pl.CostEstimate(flops=0, bytes_accessed=8 * 1000 * 1000, transcendentals=0),
        name="quantize_right",
    )(zy, first, second)


def combine(left_parts, right_part):
    return pl.pallas_call(
        combine_kernel,
        out_shape=jax.ShapeDtypeStruct((512, 128), f32),
        in_specs=vmem_specs(2),
        out_specs=vmem_specs(1)[0],
        name="combine",
    )(left_parts, right_part)


def combine_right(parts):
    return pl.pallas_call(
        combine_right_kernel,
        out_shape=jax.ShapeDtypeStruct((528, 128), jnp.int16),
        in_specs=vmem_specs(len(parts)),
        out_specs=vmem_specs(1)[0],
        cost_estimate=pl.CostEstimate(flops=0, bytes_accessed=6 * 1000 * 1000, transcendentals=0),
        name="combine_right",
    )(*parts)


def overlap_kernel(core_ref, own_ref, other_ref, phi_ref, x_ref, out_ref, same_ref, cross_ref):
    keep = (lax.broadcasted_iota(jnp.int32, (G, 128), 1) < G) == (core_ref[0] == 0)
    same_ref[...] = jnp.zeros_like(same_ref)
    cross_ref[...] = jnp.zeros_like(cross_ref)

    def rows_block(i, carry):
        rows = pl.ds(pl.multiple_of(i * G, G), G)
        value = jnp.where(keep, own_ref[rows], pltpu.roll(other_ref[rows], G, 1))
        turned = pltpu.roll(value, G, 1)
        x_ref[rows] = value
        for o in range(COUPLES):
            phi = phi_ref[o, rows].astype(f32)
            same_ref[o] += jnp.sum((phi * value).reshape(8, 8, 128), axis=0)
            cross_ref[o] += jnp.sum((phi * turned).reshape(8, 8, 128), axis=0)
        return carry

    lax.fori_loop(0, 8, rows_block, 0)
    out_ref[pl.ds(0, COUPLES)] = jnp.sum(same_ref[...], axis=1)
    out_ref[pl.ds(COUPLES, COUPLES)] = jnp.sum(cross_ref[...], axis=1)


def project_kernel(x_ref, phi_ref, over0_ref, over1_ref, over2_ref, over3_ref, out_ref, coef_ref):
    lane = lax.broadcasted_iota(jnp.int32, (COUPLES, 128), 1)
    for k in range(2):
        half = pl.ds(k * COUPLES, COUPLES)
        part = (over0_ref[half] + over2_ref[half]) + (over1_ref[half] + over3_ref[half])
        low = jnp.sum(jnp.where(lane < G, part, 0.0), axis=1, keepdims=True)
        high = jnp.sum(jnp.where(lane < G, 0.0, part), axis=1, keepdims=True)
        coef_ref[k] = jnp.where(lane < G, low, high) / CELLS

    def rows_block(i, carry):
        rows = pl.ds(pl.multiple_of(i * G, G), G)
        same = jnp.zeros((G, 128), f32)
        cross = jnp.zeros((G, 128), f32)
        for o in range(COUPLES):
            phi = phi_ref[o, rows].astype(f32)
            same = same + phi * coef_ref[0, o : o + 1]
            cross = cross + phi * coef_ref[1, o : o + 1]
        out_ref[rows] = x_ref[rows] - same - pltpu.roll(cross, G, 1)
        return carry

    lax.fori_loop(0, 8, rows_block, 0)


def vmem_specs(n):
    return [pl.BlockSpec(memory_space=pltpu.VMEM)] * n


def smem_specs(n):
    return [pl.BlockSpec(memory_space=pltpu.SMEM)] * n


def lane_exchange(mine, core):
    other = lax.ppermute(mine, "core", [(0, 1), (1, 0)])
    lane = lax.broadcasted_iota(jnp.int32, mine.shape, mine.ndim - 1)
    return jnp.where((lane < G) == (core == 0), mine, jnp.roll(other, G, axis=-1))


def home():
    pairs = []
    for z in range(NZ):
        for q in range(NY):
            y, b = z // 2, z % 2
            holder = (2 * y + (q + 1 if b else -q)) % NZ
            pairs.append((holder * NY + y, z * NY + q))
    return pairs


def ring(size, step):
    return [(i, (i + step) % size) for i in range(size)]


def over_y(value):
    return [value] + [lax.ppermute(value, "y", ring(NY, k)) for k in range(1, NY)]


def local(orbitals, pair_table):
    z, x, y, core = (lax.axis_index(a) for a in ("z", "x", "y", "core"))
    mine = orbitals[0]
    slots = packed_slots(pair_table[:, 0], pair_table[:, 1], pair_table[:, 2])
    slots = lax.all_gather(slots[None], ("z", "x"), axis=0, tiled=True)
    z_couples = lax.all_gather(mine.reshape(1, 512, 128), "z", axis=0, tiled=True)
    own = lane_exchange(mine, core)
    spread = jnp.broadcast_to(own[None], (NX * NY,) + own.shape)
    left = lax.all_to_all(spread, ("x", "y"), split_axis=0, concat_axis=0, tiled=True)

    z_couples, left, slots = lax.optimization_barrier((z_couples, left, slots))
    me = (z * 16 + x * 4 + y).astype(jnp.int32).reshape(1)
    tasks = pl.pallas_call(
        assign_kernel,
        out_shape=jax.ShapeDtypeStruct((18,), jnp.int32),
        in_specs=smem_specs(2),
        out_specs=pl.BlockSpec(memory_space=pltpu.SMEM),
        scratch_shapes=[pltpu.SMEM((NZ * NX * NY,), jnp.int32)],
        cost_estimate=pl.CostEstimate(flops=0, bytes_accessed=60 * 1000 * 1000, transcendentals=0),
        name="assign",
    )(me, slots)
    phi_all = lax.all_gather(z_couples, "x", axis=0, tiled=True)
    right = lax.all_to_all(z_couples, "y", split_axis=0, concat_axis=0, tiled=True)
    right, tasks = lax.optimization_barrier((right, tasks))
    right_other = lax.ppermute(right, "core", ring(2, 1))
    ids = jnp.stack([core, y]).astype(jnp.int32)

    w_depth, w_rows, w_planes = (jnp.asarray(w) for w in weights())
    left_parts, sacc, cacc = pl.pallas_call(
        pairs_kernel,
        out_shape=(
            jax.ShapeDtypeStruct((NX * NY, 528, 128), jnp.int16),
            jax.ShapeDtypeStruct((2, ROWS, 128), f32),
            jax.ShapeDtypeStruct((2, ROWS, 128), f32),
        ),
        in_specs=smem_specs(2) + vmem_specs(7),
        out_specs=tuple(vmem_specs(3)),
        scratch_shapes=[
            pltpu.VMEM((ROWS, 128), f32),
            pltpu.VMEM((2, ROWS, 128), bf16),
            pltpu.VMEM((2, ROWS, 128), bf16),
            pltpu.VMEM((4, ROWS, 128), f32),
        ],
        compiler_params=pltpu.CompilerParams(vmem_limit_bytes=48 * 1024 * 1024),
        cost_estimate=pl.CostEstimate(flops=0, bytes_accessed=60 * 1000 * 1000, transcendentals=0),
        name="pairs",
    )(
        ids,
        tasks,
        left.reshape(4, ROWS, 128),
        right,
        right_other,
        w_depth,
        w_rows,
        w_planes,
        coulomb(),
    )

    other = lax.ppermute(cacc, "core", ring(2, 1))
    right_parts = quantize_right(jnp.stack([z, y]).astype(jnp.int32), sacc.reshape(NZ, 512, 128), other.reshape(NZ, 512, 128))
    left_parts = lax.all_to_all(left_parts, ("x", "y"), split_axis=0, concat_axis=0, tiled=True)
    right_parts = [
        lax.ppermute(part, "z", ring(NZ, k)) if k else part for k, part in enumerate(right_parts)
    ]
    from_right = lax.ppermute(combine_right(right_parts), ("z", "y"), home())
    action = combine(left_parts, from_right)
    action_other = lax.ppermute(action, "core", ring(2, 1))

    slab_action, over = pl.pallas_call(
        overlap_kernel,
        out_shape=(
            jax.ShapeDtypeStruct((512, 128), f32),
            jax.ShapeDtypeStruct((2 * COUPLES, 128), f32),
        ),
        in_specs=smem_specs(1) + vmem_specs(3),
        out_specs=tuple(vmem_specs(2)),
        scratch_shapes=[pltpu.VMEM((COUPLES, 8, 128), f32)] * 2,
        name="overlap",
    )(ids, action, action_other, phi_all)
    out = pl.pallas_call(
        project_kernel,
        out_shape=jax.ShapeDtypeStruct((512, 128), f32),
        in_specs=vmem_specs(2 + NY),
        out_specs=vmem_specs(1)[0],
        scratch_shapes=[pltpu.VMEM((2, COUPLES, 128), f32)],
        name="project",
    )(slab_action, phi_all, *over_y(over + lax.ppermute(over, "core", ring(2, 1))))
    return out.reshape(1, 8, G, 128)


def solution(mesh):
    grid = Mesh(mesh.devices.reshape(NZ, NX, NY, 2), ("z", "x", "y", "core"))
    placed = (P(("z", "x"), ("y", "core"), None, None), P(("z", "x"), None))
    return jax.shard_map(
        local,
        mesh=grid,
        in_specs=placed,
        out_specs=P(("z", "x"), ("y", "core"), None, None),
        check_vma=False,
    )
```
